32 devices in a mesh: outer: 4 (over z), inner: 8 (over y, x, core).
Axes of the slice: x: 2, y: 2, z: 4, core: 2. Of those that a mesh axis runs over, the one named last changes fastest.
Arguments:
- query_rot: bfloat16 [4, 1024, 896], P('outer', 'inner'), may hold values from -6 to 6
- key_rot: bfloat16 [4, 1024, 128], P('outer', 'inner'), may hold values from -6 to 6
- value_rows: bfloat16 [4, 1024, 128], P('outer', 'inner'), may hold values from -6 to 6
- attention_out: bfloat16 [4, 1024, 896], P('outer', 'inner'), may hold values from -6 to 6
- grad_out: bfloat16 [4, 1024, 896], P('outer', 'inner'), may hold values from -12 to 12
- log_norm: float32 [4, 7, 1024], P('outer', None, 'inner'), may hold values from 7.5 to 9
- segments: int32 [1, 1024], P(None, 'inner'), may hold values from 0 to 2, as said below
- block_table: int32 [1, 8, 8], P(None, 'inner'), may hold values from 0 to 1, as said below
Outputs:
- grad_query: bfloat16 [4, 1024, 896], P('outer', 'inner')
- grad_key: bfloat16 [4, 1024, 128], P('outer', 'inner')
- grad_value: bfloat16 [4, 1024, 128], P('outer', 'inner')
- grad_bias: float32 [4608], replicated
The draws below stay inside these ranges and needn't reach their ends.
Inputs may be any that keep to these rules, and one draw needn't show every extreme that they name: `segments`: in every example the tokens of segment 0 come first, then those of segment 1, then those of segment 2; each segment is present. block_table[e,a,b] is 1 exactly when some token of block a (tokens a * 128 to a * 128 + 127) and some token of block b of example e have segments s_q and s_k with s_k == 0 or s_k == s_q, else 0.
All inputs are finite; a program needn't handle non-finite values.
Results may differ from the reference program's by a relative error of at most 0.0056.
Values may be sent and summed in bfloat16 or wider, within the bound.
A program may use at most 64 MiB of HBM per device.

```python
import math
import jax
import jax.numpy as jnp
from jax import lax

TOK_DEV = 128
HEADS = 28
KV_HEADS = 4
HEAD_DIM = 128
GROUP = 7
SEQ = 1024
BLOCKS = 8
PAIRS = 4
EXAMPLES = 1


def layout_helper(key):
    base = jax.random.fold_in(key, 7)
    example_keys = jax.random.split(base, EXAMPLES)

    def one_layout(example_key):
        first_key, second_key = jax.random.split(example_key)
        shortest = SEQ // 16
        longest = SEQ // 4 + 1
        chosen = jax.random.randint(first_key, (), shortest, longest)
        rejected = jax.random.randint(second_key, (), shortest, longest)
        positions = jnp.arange(SEQ)
        prompt = SEQ - chosen - rejected
        return jnp.where(positions < prompt, 0, jnp.where(positions < prompt + chosen, 1, 2)).astype(jnp.int32)
    return jax.vmap(one_layout)(example_keys)


def draw_segments(key, part):
    return layout_helper(key)


def draw_block_table(key, part):
    layout = layout_helper(key).reshape(EXAMPLES, BLOCKS, TOK_DEV)
    present = jnp.stack([jnp.any(layout == 0, axis=-1), jnp.any(layout == 1, axis=-1), jnp.any(layout == 2, axis=-1)], axis=-1)
    query_side = present[:, :, None, :]
    key_side = present[:, None, :, :]
    any_query = jnp.any(query_side, axis=-1)
    allowed = key_side[..., 0] & any_query | query_side[..., 1] & key_side[..., 1] | query_side[..., 2] & key_side[..., 2]
    return allowed.astype(jnp.int32)


def block_scale(stream_key, extent, cuts, smallest, high):
    def one(axis_at, shards_of):
        steps = jax.random.uniform(jax.random.fold_in(jax.random.fold_in(stream_key, 6), axis_at), (shards_of,), jnp.float32, smallest / len(cuts), high / len(cuts))
        return jnp.repeat(jnp.exp(steps), extent[axis_at] // shards_of).reshape((-1,) + (1,) * (len(extent) - axis_at - 1))

    level = one(*cuts[0])
    for cut in cuts[1:]:
        level = level * one(*cut)
    return level


def scatter_about(stream_key, shape, spread, limit, cuts=(), held_as=jnp.bfloat16):
    drawn = jax.random.normal(stream_key, shape, jnp.float32) * spread
    if len(cuts) > 0:
        drawn = block_scale(stream_key, shape, cuts, -0.22, 0.18) * drawn
    return jnp.clip(drawn, min=-limit, max=limit).astype(held_as)


def setup_inputs(seed: int = 0) -> dict:
    arg_keys = jax.random.split(jax.random.key(seed), 9)
    query_rot = scatter_about(arg_keys[0], (PAIRS, SEQ, GROUP * HEAD_DIM), 1.0, 6.0, ((0, 4), (1, 8)))
    key_rot = scatter_about(arg_keys[1], (PAIRS, SEQ, HEAD_DIM), 1.0, 6.0, ((0, 4), (1, 8)))
    value_rows = scatter_about(arg_keys[2], (PAIRS, SEQ, HEAD_DIM), 1.0, 6.0, ((0, 4), (1, 8)))
    attention_out = scatter_about(arg_keys[3], (PAIRS, SEQ, GROUP * HEAD_DIM), 1.0, 6.0, ((0, 4), (1, 8)))
    grad_out = jnp.clip(jax.random.uniform(arg_keys[4], (PAIRS, SEQ, GROUP * HEAD_DIM), jnp.float32, -12.0, 12.0) * block_scale(arg_keys[4], (PAIRS, SEQ, GROUP * HEAD_DIM), ((0, 4), (1, 8)), -0.4, 0.0), -12.0, 12.0).astype(jnp.bfloat16)
    log_norm = jnp.clip(7.5 + 1.5 * jax.random.uniform(arg_keys[5], (PAIRS, GROUP, SEQ), jnp.float32) ** block_scale(arg_keys[5], (PAIRS, GROUP, SEQ), ((0, 4), (2, 8)), -0.2, 0.2), 7.5, 9.0)
    segments = draw_segments(jax.random.fold_in(arg_keys[8], 71), 0)
    block_table = draw_block_table(jax.random.fold_in(arg_keys[8], 71), 0)
    return {"query_rot": query_rot, "key_rot": key_rot, "value_rows": value_rows, "attention_out": attention_out, "grad_out": grad_out, "log_norm": log_norm, "segments": segments, "block_table": block_table}


ROPE_BASE = 1000000.0


def unrotate(gradient, positions, heads):
    rows_here = gradient.shape[0]
    halfway = HEAD_DIM // 2
    per_head = gradient.reshape(rows_here, heads, HEAD_DIM)
    frequency = jnp.exp(jnp.arange(halfway, dtype=jnp.float32) * (-2.0 * math.log(ROPE_BASE) / HEAD_DIM))
    angles = positions[:, None] * frequency[None, :]
    cosine = jnp.cos(angles)[:, None, :]
    sine_term = jnp.sin(angles)[:, None, :]
    first_half = per_head[..., :halfway]
    second_half = per_head[..., halfway:]
    joined = jnp.concatenate([first_half * cosine + second_half * sine_term, second_half * cosine - first_half * sine_term], axis=-1)
    return joined.reshape(rows_here, heads * HEAD_DIM)


def one_pair(inputs):
    query_rot, key_rot, value_rows, attention_out, grad_out, log_norm, segments, block_table = inputs
    group_size = HEADS // KV_HEADS
    scaling = HEAD_DIM ** -0.5
    highest = lax.Precision.HIGHEST
    queries = query_rot.astype(jnp.float32).reshape(SEQ, group_size, HEAD_DIM)
    grads_out = grad_out.astype(jnp.float32).reshape(SEQ, group_size, HEAD_DIM)
    outputs = attention_out.astype(jnp.float32).reshape(SEQ, group_size, HEAD_DIM)
    keys_all = key_rot.astype(jnp.float32)
    values_all = value_rows.astype(jnp.float32)
    deltas = jnp.transpose(jnp.sum(grads_out * outputs, axis=-1), (1, 0))

    def one_block(carry, block_index):
        key_grads, value_grads = carry
        start = (block_index * TOK_DEV).astype(jnp.int32)
        block_queries = lax.dynamic_slice_in_dim(queries, start, TOK_DEV, 0)
        block_grads = lax.dynamic_slice_in_dim(grads_out, start, TOK_DEV, 0)
        seg_query = lax.dynamic_slice_in_dim(segments, start, TOK_DEV, 0)
        block_norms = lax.dynamic_slice_in_dim(log_norm, start, TOK_DEV, 1)
        block_deltas = lax.dynamic_slice_in_dim(deltas, start, TOK_DEV, 1)
        table_row = jnp.repeat(lax.dynamic_index_in_dim(block_table, block_index.astype(jnp.int32), 0, keepdims=False), TOK_DEV)
        allowed = (table_row[None, :] == 1) & ((segments[None, :] == 0) | (segments[None, :] == seg_query[:, None]))
        scores = jnp.einsum("tgd,ud->gtu", block_queries, keys_all, precision=highest) * scaling
        probs = jnp.where(allowed[None], jnp.exp(scores - block_norms[..., None]), 0.0)
        probs_low = lax.optimization_barrier(probs.astype(jnp.bfloat16)).astype(jnp.float32)
        grad_probs = jnp.einsum("tgd,ud->gtu", block_grads, values_all, precision=highest)
        grad_scores = probs * (grad_probs - block_deltas[..., None])
        scores_low = lax.optimization_barrier(grad_scores.astype(jnp.bfloat16)).astype(jnp.float32)
        value_grads = value_grads + jnp.einsum("gtu,tgd->ud", probs_low, block_grads, precision=highest)
        key_grads = key_grads + jnp.einsum("gtu,tgd->ud", scores_low, block_queries, precision=highest)
        query_part = jnp.einsum("gtu,ud->tgd", scores_low, keys_all, precision=highest)
        return (key_grads, value_grads), query_part

    empty = jnp.zeros((SEQ, HEAD_DIM), jnp.float32)
    (key_grads, value_grads), query_blocks = lax.scan(one_block, (empty, empty), jnp.arange(BLOCKS, dtype=jnp.int32))
    positions = jnp.arange(SEQ, dtype=jnp.float32)
    query_full = unrotate(query_blocks.reshape(SEQ, group_size * HEAD_DIM) * scaling, positions, group_size)
    key_full = unrotate(key_grads * scaling, positions, 1)
    value_full = value_grads
    return (query_full.astype(jnp.bfloat16), key_full.astype(jnp.bfloat16), value_full.astype(jnp.bfloat16), jnp.sum(query_full, axis=0), jnp.sum(key_full, axis=0), jnp.sum(value_full, axis=0))


def reference(query_rot, key_rot, value_rows, attention_out, grad_out, log_norm, segments, block_table):
    seg_pairs = jnp.repeat(segments, KV_HEADS, axis=0)
    table_pairs = jnp.repeat(block_table, KV_HEADS, axis=0)
    results = lax.map(one_pair, (query_rot, key_rot, value_rows, attention_out, grad_out, log_norm, seg_pairs, table_pairs))
    query_bias = jnp.sum(results[3].reshape(EXAMPLES, HEADS * HEAD_DIM), axis=0)
    key_bias = jnp.sum(results[4].reshape(EXAMPLES, KV_HEADS * HEAD_DIM), axis=0)
    value_bias = jnp.sum(results[5].reshape(EXAMPLES, KV_HEADS * HEAD_DIM), axis=0)
    return (results[0], results[1], results[2], jnp.concatenate([query_bias, key_bias, value_bias]))
```

```python
import functools
import math

import jax
import jax.numpy as jnp
from jax import lax
from jax.experimental import pallas as pl
from jax.experimental.pallas import tpu as pltpu
from jax.sharding import PartitionSpec as P

HEADS = 28
KV_HEADS = 4
HEAD_DIM = 128
GROUP = HEADS // KV_HEADS
ROPE_BASE = 1000000.0
ROOT = math.sqrt(HEAD_DIM)
SCALE = 1.0 / ROOT
EXP2_SCALE = math.log2(math.e) / ROOT
MASKED = -1e30
EXTRA = 16
BIAS_ROWS = 16
MESH = pl.DeviceIdType.MESH
F32 = jnp.float32
BF16 = jnp.bfloat16


def partner(index, step, count):
    result = 0
    bit = 1
    while bit < count:
        result = result + ((index // bit + step // bit) % 2) * bit
        bit *= 2
    return result


def pieces(x):
    high = x.astype(BF16).astype(F32)
    rest = x - high
    middle = rest.astype(BF16).astype(F32)
    return high, middle, rest - middle


def dot(a, b):
    return jnp.dot(a, b, preferred_element_type=F32)


def kernel(
    inners, outers, q_ref, k_ref, v_ref, ao_ref, go_ref, norm_ref, seg_ref,
    dq_ref, dk_ref, dv_ref, bias_ref,
    kv, q_aug, go_aug, q_t, go_t, probs, grads, dq_acc, own_acc, part_out, part_in,
    bias_own, bias_in, plane_own, plane_in,
    kv_send, kv_recv, part_send, part_recv, bias_send, bias_recv, plane_send, plane_recv,
):
    tokens = k_ref.shape[0]
    rows = GROUP * tokens
    me = lax.axis_index("inner")
    plane = lax.axis_index("outer")

    def inner_id(step):
        return (plane, partner(me, step, inners))

    def outer_id(step):
        return (partner(plane, step, outers), me)

    barrier = pltpu.get_barrier_semaphore()
    for step in range(1, inners):
        pl.semaphore_signal(barrier, inc=1, device_id=inner_id(step), device_id_type=MESH)
    for step in range(1, outers):
        pl.semaphore_signal(barrier, inc=1, device_id=outer_id(step), device_id_type=MESH)

    seg = seg_ref[...].astype(F32)
    row = lax.broadcasted_iota(jnp.int32, (EXTRA, tokens), 0)
    seg_rows = jnp.broadcast_to(seg, (EXTRA, tokens))
    extra = jnp.where(row < 3, 1.0, 0.0)
    extra = jnp.where((row == 3) & (seg_rows == 1.0), 1.0, extra)
    extra = jnp.where((row == 4) & (seg_rows == 2.0), 1.0, extra)
    kv[0, :HEAD_DIM] = jnp.transpose(v_ref[...])
    kv[0, HEAD_DIM : 2 * HEAD_DIM] = jnp.transpose(k_ref[...])
    kv[0, 2 * HEAD_DIM : 2 * HEAD_DIM + EXTRA] = extra.astype(BF16)
    for slot in range(inners):
        kv[slot, 2 * HEAD_DIM + EXTRA :] = jnp.zeros((HEAD_DIM - EXTRA, tokens), BF16)

    pl.semaphore_wait(barrier, inners + outers - 2)

    sent = 2 * HEAD_DIM + EXTRA

    def kv_copy(step):
        return pltpu.make_async_remote_copy(
            src_ref=kv.at[0, pl.ds(0, sent)],
            dst_ref=kv.at[step, pl.ds(0, sent)],
            send_sem=kv_send.at[step],
            recv_sem=kv_recv.at[step],
            device_id=inner_id(step),
            device_id_type=MESH,
        )

    def part_copy(step):
        return pltpu.make_async_remote_copy(
            src_ref=part_out.at[step],
            dst_ref=part_in.at[step],
            send_sem=part_send.at[step],
            recv_sem=part_recv.at[step],
            device_id=inner_id(step),
            device_id_type=MESH,
        )

    for step in range(1, inners):
        kv_copy(step).start()

    norms = norm_ref[...] * -ROOT
    high, middle, low = pieces(norms)
    row8 = lax.broadcasted_iota(jnp.int32, (8, tokens), 0)
    seg8 = jnp.broadcast_to(seg, (8, tokens))
    masks = jnp.where((row8 == 3) & (seg8 != 1.0), MASKED, 0.0)
    masks = jnp.where((row8 == 4) & (seg8 != 2.0), MASKED, masks)
    lane = lax.broadcasted_iota(jnp.int32, (tokens, HEAD_DIM), 1)
    for g in range(GROUP):
        here = slice(g * tokens, (g + 1) * tokens)
        cols = slice(g * HEAD_DIM, (g + 1) * HEAD_DIM)
        query = q_ref[:, cols]
        grad = go_ref[:, cols]
        q_aug[here, :HEAD_DIM] = query
        go_aug[here, :HEAD_DIM] = grad
        q_t[:, here] = jnp.transpose(query)
        go_t[:, here] = jnp.transpose(grad)
        top = jnp.where(row8 == 0, high[g : g + 1], masks)
        top = jnp.where(row8 == 1, middle[g : g + 1], top)
        top = jnp.where(row8 == 2, low[g : g + 1], top)
        full = jnp.concatenate([top, jnp.zeros((HEAD_DIM - 8, tokens), F32)], axis=0)
        q_aug[here, HEAD_DIM:] = jnp.transpose(full).astype(BF16)
        delta = -jnp.sum(
            grad.astype(F32) * ao_ref[:, cols].astype(F32), axis=1, keepdims=True
        )
        d_high, d_middle, d_low = pieces(delta)
        side = jnp.where(lane == 0, d_high, 0.0)
        side = jnp.where(lane == 1, d_middle, side)
        side = jnp.where(lane == 2, d_low, side)
        go_aug[here, HEAD_DIM:] = side.astype(BF16)

    half = HEAD_DIM // 2
    spot = lax.broadcasted_iota(jnp.int32, (tokens, HEAD_DIM), 0) + me * tokens
    frequency = jnp.exp((lane % half).astype(F32) * (-2.0 * math.log(ROPE_BASE) / HEAD_DIM))
    waves = jnp.sin(spot.astype(F32) * frequency + jnp.where(lane < half, 0.0, math.pi / 2))
    turned = pltpu.roll(waves, half, 1)
    cosine = jnp.where(lane < half, turned, waves)
    sine = jnp.where(lane < half, waves, -turned)

    def unrotate(x):
        return x * cosine + pltpu.roll(x, half, 1) * sine

    chunk = 256
    starts = list(range(0, rows, chunk))

    def compute(g, first):
        block = jnp.concatenate([kv[2 * g], kv[2 * g + 1]], axis=1)
        values_t = jnp.concatenate([block[:HEAD_DIM], block[2 * HEAD_DIM :]], axis=0)
        keys_t = block[HEAD_DIM:]
        keys = jnp.transpose(block[HEAD_DIM : 2 * HEAD_DIM])
        for start in starts:
            here = slice(start, min(start + chunk, rows))
            scores = dot(q_aug[here], keys_t)
            chances = jnp.exp2(scores * EXP2_SCALE)
            probs[here] = chances.astype(BF16)
            low_grads = (chances * dot(go_aug[here], values_t)).astype(BF16)
            grads[here] = low_grads
            part = dot(low_grads, keys)
            if first:
                dq_acc[here] = part
            else:
                dq_acc[here] += part
        value_part = dot(go_t[...], probs[...])
        key_part = dot(q_t[...], grads[...])
        return key_part, value_part

    def put(slot, key_part, value_part):
        part_out[slot, :HEAD_DIM] = key_part.astype(BF16)
        part_out[slot, HEAD_DIM:] = value_part.astype(BF16)
        part_copy(slot).start()

    kv_copy(1).wait_recv()
    key_part, value_part = compute(0, True)
    own_acc[:HEAD_DIM] = key_part[:, :tokens]
    own_acc[HEAD_DIM:] = value_part[:, :tokens]
    put(1, key_part[:, tokens:], value_part[:, tokens:])

    def turn(g, carry):
        kv_copy(2 * g).wait_recv()
        kv_copy(2 * g + 1).wait_recv()
        key_part, value_part = compute(g, False)
        put(2 * g, key_part[:, :tokens], value_part[:, :tokens])
        put(2 * g + 1, key_part[:, tokens:], value_part[:, tokens:])
        return carry

    groups = inners // 2
    if groups <= 4:
        for g in range(1, groups):
            turn(g, 0)
    else:
        lax.fori_loop(1, groups, turn, 0)

    bias_own[...] = jnp.zeros((BIAS_ROWS, HEAD_DIM), F32)
    for g in range(GROUP):
        full = unrotate(dq_acc[g * tokens : (g + 1) * tokens] * SCALE)
        dq_ref[:, g * HEAD_DIM : (g + 1) * HEAD_DIM] = full.astype(BF16)
        bias_own[g : g + 1] = jnp.sum(full, axis=0, keepdims=True)

    total = own_acc[...]
    for step in range(1, inners):
        part_copy(step).wait_recv()
        total = total + part_in[step].astype(F32)
    key_full = unrotate(jnp.transpose(total[:HEAD_DIM]) * SCALE)
    value_full = jnp.transpose(total[HEAD_DIM:])
    dk_ref[...] = key_full.astype(BF16)
    dv_ref[...] = value_full.astype(BF16)
    bias_own[GROUP : GROUP + 1] = jnp.sum(key_full, axis=0, keepdims=True)
    bias_own[GROUP + 1 : GROUP + 2] = jnp.sum(value_full, axis=0, keepdims=True)

    def bias_copy(step, slot):
        return pltpu.make_async_remote_copy(
            src_ref=bias_own,
            dst_ref=bias_in.at[slot],
            send_sem=bias_send.at[step],
            recv_sem=bias_recv.at[step],
            device_id=inner_id(step),
            device_id_type=MESH,
        )

    def plane_copy(step, slot):
        return pltpu.make_async_remote_copy(
            src_ref=plane_own,
            dst_ref=plane_in.at[slot],
            send_sem=plane_send.at[step],
            recv_sem=plane_recv.at[step],
            device_id=outer_id(step),
            device_id_type=MESH,
        )

    for step in range(1, inners):
        bias_copy(step, me).start()
    bias_in[me] = bias_own[...]
    for step in range(1, inners):
        bias_copy(step, partner(me, step, inners)).wait_recv()
    summed = bias_in[0]
    for slot in range(1, inners):
        summed = summed + bias_in[slot]
    plane_own[...] = summed
    for step in range(1, outers):
        plane_copy(step, plane).start()
    plane_in[plane] = summed
    for step in range(1, outers):
        plane_copy(step, partner(plane, step, outers)).wait_recv()
    for head in range(KV_HEADS):
        whole = plane_in[head]
        for other in range(head + KV_HEADS, outers, KV_HEADS):
            whole = whole + plane_in[other]
        bias_ref[head * GROUP : (head + 1) * GROUP] = whole[:GROUP]
        bias_ref[HEADS + head : HEADS + head + 1] = whole[GROUP : GROUP + 1]
        at = HEADS + KV_HEADS + head
        bias_ref[at : at + 1] = whole[GROUP + 1 : GROUP + 2]

    for step in range(1, inners):
        kv_copy(step).wait_send()
        part_copy(step).wait_send()
        bias_copy(step, me).wait_send()
    for step in range(1, outers):
        plane_copy(step, plane).wait_send()


def local(inners, outers, query_rot, key_rot, value_rows, attention_out, grad_out, log_norm,
          segments, block_table):
    del block_table
    tokens = query_rot.shape[1]
    rows = GROUP * tokens
    if segments.shape[0] > 1:
        example = lax.axis_index("outer") // KV_HEADS
        segments = lax.dynamic_slice_in_dim(segments, example, 1, 0)
    vmem = pl.BlockSpec(memory_space=pltpu.VMEM)
    sems = pltpu.SemaphoreType.DMA
    outs = pl.pallas_call(
        functools.partial(kernel, inners, outers),
        out_shape=(
            jax.ShapeDtypeStruct((tokens, GROUP * HEAD_DIM), BF16),
            jax.ShapeDtypeStruct((tokens, HEAD_DIM), BF16),
            jax.ShapeDtypeStruct((tokens, HEAD_DIM), BF16),
            jax.ShapeDtypeStruct((HEADS + 2 * KV_HEADS, HEAD_DIM), F32),
        ),
        in_specs=[vmem] * 7,
        out_specs=(vmem,) * 4,
        scratch_shapes=[
            pltpu.VMEM((inners, 3 * HEAD_DIM, tokens), BF16),
            pltpu.VMEM((rows, 2 * HEAD_DIM), BF16),
            pltpu.VMEM((rows, 2 * HEAD_DIM), BF16),
            pltpu.VMEM((HEAD_DIM, rows), BF16),
            pltpu.VMEM((HEAD_DIM, rows), BF16),
            pltpu.VMEM((rows, 2 * tokens), BF16),
            pltpu.VMEM((rows, 2 * tokens), BF16),
            pltpu.VMEM((rows, HEAD_DIM), F32),
            pltpu.VMEM((2 * HEAD_DIM, tokens), F32),
            pltpu.VMEM((inners, 2 * HEAD_DIM, tokens), BF16),
            pltpu.VMEM((inners, 2 * HEAD_DIM, tokens), BF16),
            pltpu.VMEM((BIAS_ROWS, HEAD_DIM), F32),
            pltpu.VMEM((inners, BIAS_ROWS, HEAD_DIM), F32),
            pltpu.VMEM((BIAS_ROWS, HEAD_DIM), F32),
            pltpu.VMEM((outers, BIAS_ROWS, HEAD_DIM), F32),
            sems((inners,)), sems((inners,)), sems((inners,)), sems((inners,)),
            sems((inners,)), sems((inners,)), sems((outers,)), sems((outers,)),
        ],
        compiler_params=pltpu.CompilerParams(
            collective_id=0, has_side_effects=True, vmem_limit_bytes=48 * 1024 * 1024
        ),
        name="attention_backward",
    )(query_rot[0], key_rot[0], value_rows[0], attention_out[0], grad_out[0], log_norm[0], segments)
    return outs[0][None], outs[1][None], outs[2][None], outs[3].reshape(-1)


def solution(mesh):
    placed = (
        P("outer", "inner", None),
        P("outer", "inner", None),
        P("outer", "inner", None),
        P("outer", "inner", None),
        P("outer", "inner", None),
        P("outer", None, "inner"),
        P(None, "inner"),
        P(None, "inner", None),
    )
    return jax.shard_map(
        functools.partial(local, mesh.shape["inner"], mesh.shape["outer"]),
        mesh=mesh,
        in_specs=placed,
        out_specs=(
            P("outer", "inner", None),
            P("outer", "inner", None),
            P("outer", "inner", None),
            P(),
        ),
        check_vma=False,
    )
```

```python
import functools
import math

import jax
import jax.numpy as jnp
import numpy as np
from jax import lax
from jax.experimental import pallas as pl
from jax.experimental.pallas import tpu as pltpu
from jax.sharding import PartitionSpec as P

HEADS = 28
KV_HEADS = 4
HEAD_DIM = 128
GROUP = HEADS // KV_HEADS
ROPE_BASE = 1000000.0
ROOT = math.sqrt(HEAD_DIM)
SCALE = 1.0 / ROOT
EXP2_SCALE = math.log2(math.e) / ROOT
MASKED = -1e30
EXTRA = 16
BIAS_ROWS = 16
VMEM_LIMIT = 63 * 1024 * 1024
MESH = pl.DeviceIdType.MESH
F32 = jnp.float32
BF16 = jnp.bfloat16


def partner(index, step, count):
    result = 0
    bit = 1
    while bit < count:
        result = result + ((index // bit + step // bit) % 2) * bit
        bit *= 2
    return result


def pieces(x):
    high = x.astype(BF16).astype(F32)
    rest = x - high
    middle = rest.astype(BF16).astype(F32)
    return high, middle, rest - middle


def dot(a, b):
    return jnp.dot(a, b, preferred_element_type=F32)


def kernel(
    inners, outers, k_hbm, v_hbm, seg_hbm, q_hbm, go_hbm, ao_hbm, norm_hbm, base_hbm, starts_hbm,
    dq_hbm, dk_hbm, dv_hbm, bias_hbm,
    k_ref, v_ref, seg_ref, q_ref, go_ref, ao_ref, norm_ref, base_ref, starts_ref, load_sem,
    dq_ref, dk_ref, dv_ref, bias_ref, store_sem,
    kv, q_aug, go_aug, q_t, go_t, probs, grads, dq_acc, own_acc, part_out, part_in,
    sums, angles, bias_own, bias_in, plane_own, plane_in,
    kv_send, kv_recv, part_send, part_recv, bias_send, bias_recv, plane_send, plane_recv,
):
    tokens = k_ref.shape[0]
    rows = GROUP * tokens
    me = lax.axis_index("inner")
    plane = lax.axis_index("outer")

    loads = [
        pltpu.make_async_copy(source, target, load_sem.at[i])
        for i, (source, target) in enumerate([
            (k_hbm, k_ref), (v_hbm, v_ref), (seg_hbm, seg_ref), (q_hbm, q_ref), (go_hbm, go_ref),
            (ao_hbm, ao_ref), (norm_hbm, norm_ref), (base_hbm, base_ref), (starts_hbm, starts_ref),
        ])
    ]
    for load in loads:
        load.start()
    stores = [
        pltpu.make_async_copy(source, target, store_sem.at[i])
        for i, (source, target) in enumerate([
            (dq_ref, dq_hbm), (dk_ref, dk_hbm), (dv_ref, dv_hbm), (bias_ref, bias_hbm),
        ])
    ]

    def inner_id(step):
        return (plane, partner(me, step, inners))

    def outer_id(step):
        return (partner(plane, step, outers), me)

    barrier = pltpu.get_barrier_semaphore()
    for step in range(1, inners):
        pl.semaphore_signal(barrier, inc=1, device_id=inner_id(step), device_id_type=MESH)
    for step in range(1, outers):
        pl.semaphore_signal(barrier, inc=1, device_id=outer_id(step), device_id_type=MESH)

    for load in loads[:3]:
        load.wait()
    seg = seg_ref[...].astype(F32)
    row = lax.broadcasted_iota(jnp.int32, (EXTRA, tokens), 0)
    seg_rows = jnp.broadcast_to(seg, (EXTRA, tokens))
    extra = jnp.where(row < 3, 1.0, 0.0)
    extra = jnp.where((row == 3) & (seg_rows == 1.0), 1.0, extra)
    extra = jnp.where((row == 4) & (seg_rows == 2.0), 1.0, extra)
    kv[0, :HEAD_DIM] = jnp.transpose(v_ref[...])
    kv[0, HEAD_DIM : 2 * HEAD_DIM] = jnp.transpose(k_ref[...])
    kv[0, 2 * HEAD_DIM : 2 * HEAD_DIM + EXTRA] = extra.astype(BF16)
    for slot in range(inners):
        kv[slot, 2 * HEAD_DIM + EXTRA :] = jnp.zeros((HEAD_DIM - EXTRA, tokens), BF16)

    pl.semaphore_wait(barrier, inners + outers - 2)

    sent = 2 * HEAD_DIM + EXTRA

    def kv_copy(step):
        return pltpu.make_async_remote_copy(
            src_ref=kv.at[0, pl.ds(0, sent)],
            dst_ref=kv.at[step, pl.ds(0, sent)],
            send_sem=kv_send.at[step],
            recv_sem=kv_recv.at[step],
            device_id=inner_id(step),
            device_id_type=MESH,
        )

    def part_copy(step):
        return pltpu.make_async_remote_copy(
            src_ref=part_out.at[step],
            dst_ref=part_in.at[step],
            send_sem=part_send.at[step],
            recv_sem=part_recv.at[step],
            device_id=inner_id(step),
            device_id_type=MESH,
        )

    for step in range(1, inners):
        kv_copy(step).start()

    for load in loads[3:]:
        load.wait()
    row8 = lax.broadcasted_iota(jnp.int32, (8, tokens), 0)
    seg8 = jnp.broadcast_to(seg, (8, tokens))
    masks = jnp.where((row8 == 3) & (seg8 != 1.0), MASKED, 0.0)
    masks = jnp.where((row8 == 4) & (seg8 != 2.0), MASKED, masks)
    lane = lax.broadcasted_iota(jnp.int32, (tokens, HEAD_DIM), 1)
    for g in range(GROUP):
        here = slice(g * tokens, (g + 1) * tokens)
        cols = slice(g * HEAD_DIM, (g + 1) * HEAD_DIM)
        query = q_ref[:, cols]
        grad = go_ref[:, cols]
        q_aug[here, :HEAD_DIM] = query
        go_aug[here, :HEAD_DIM] = grad
        q_t[:, here] = jnp.transpose(query)
        go_t[:, here] = jnp.transpose(grad)
        high, middle, low = pieces(norm_ref[g] * -ROOT)
        top = jnp.where(row8 == 0, high, masks)
        top = jnp.where(row8 == 1, middle, top)
        top = jnp.where(row8 == 2, low, top)
        full = jnp.concatenate([top, jnp.zeros((HEAD_DIM - 8, tokens), F32)], axis=0)
        q_aug[here, HEAD_DIM:] = jnp.transpose(full).astype(BF16)
        delta = -jnp.sum(
            grad.astype(F32) * ao_ref[:, cols].astype(F32), axis=1, keepdims=True
        )
        d_high, d_middle, d_low = pieces(delta)
        side = jnp.where(lane == 0, d_high, 0.0)
        side = jnp.where(lane == 1, d_middle, side)
        side = jnp.where(lane == 2, d_low, side)
        go_aug[here, HEAD_DIM:] = side.astype(BF16)

    half = HEAD_DIM // 2
    for slot in range(inners):
        angles[slot : slot + 1] = starts_ref[pl.ds(partner(me, slot, inners), 1)]

    def both(table):
        below = lax.broadcasted_iota(jnp.int32, table.shape, 1) < half
        turned = pltpu.roll(table, half, 1)
        return jnp.where(below, turned, table), jnp.where(below, table, -turned)

    base_cos, base_sin = both(base_ref[...])
    start_cos, start_sin = both(angles[...])
    cosine = base_cos * start_cos[:1] - base_sin * start_sin[:1]
    sine = base_sin * start_cos[:1] + base_cos * start_sin[:1]
    base_t = jnp.transpose(base_ref[...])
    sine_t, cosine_t = base_t[:half], base_t[half:]
    sums[...] = jnp.zeros((HEAD_DIM, HEAD_DIM), F32)
    sum_lane = lax.broadcasted_iota(jnp.int32, (HEAD_DIM, HEAD_DIM), 1)

    def unrotate(x):
        return x * cosine + pltpu.roll(x, half, 1) * sine

    chunk = 256
    starts = list(range(0, rows, chunk))

    def compute(g, first):
        block = jnp.concatenate([kv[2 * g], kv[2 * g + 1]], axis=1)
        values_t = jnp.concatenate([block[:HEAD_DIM], block[2 * HEAD_DIM :]], axis=0)
        keys_t = block[HEAD_DIM:]
        keys = jnp.transpose(block[HEAD_DIM : 2 * HEAD_DIM])
        for start in starts:
            here = slice(start, min(start + chunk, rows))
            scores = dot(q_aug[here], keys_t)
            chances = jnp.exp2(scores * EXP2_SCALE)
            probs[here] = chances.astype(BF16)
            low_grads = (chances * dot(go_aug[here], values_t)).astype(BF16)
            grads[here] = low_grads
            part = dot(low_grads, keys)
            if first:
                dq_acc[here] = part
            else:
                dq_acc[here] += part
        value_part = dot(go_t[...], probs[...])
        key_part = dot(q_t[...], grads[...])
        return key_part, value_part

    def count(slot, key_part, value_part):
        upper, lower = key_part[:half], key_part[half:]
        key_sum = jnp.concatenate(
            [
                jnp.sum(upper * cosine_t + lower * sine_t, axis=1, keepdims=True),
                jnp.sum(lower * cosine_t - upper * sine_t, axis=1, keepdims=True),
            ],
            axis=0,
        )
        value_sum = jnp.sum(value_part, axis=1, keepdims=True)
        held = jnp.where(sum_lane == slot, key_sum, sums[...])
        sums[...] = jnp.where(sum_lane == half + slot, value_sum, held)

    def put(slot, key_part, value_part):
        part_out[slot, :HEAD_DIM] = key_part.astype(BF16)
        part_out[slot, HEAD_DIM:] = value_part.astype(BF16)
        part_copy(slot).start()

    kv_copy(1).wait_recv()
    key_part, value_part = compute(0, True)
    own_acc[:HEAD_DIM] = key_part[:, :tokens]
    own_acc[HEAD_DIM:] = value_part[:, :tokens]
    put(1, key_part[:, tokens:], value_part[:, tokens:])
    count(0, key_part[:, :tokens], value_part[:, :tokens])
    count(1, key_part[:, tokens:], value_part[:, tokens:])

    def turn(g, carry):
        kv_copy(2 * g).wait_recv()
        kv_copy(2 * g + 1).wait_recv()
        key_part, value_part = compute(g, False)
        put(2 * g, key_part[:, :tokens], value_part[:, :tokens])
        put(2 * g + 1, key_part[:, tokens:], value_part[:, tokens:])
        count(2 * g, key_part[:, :tokens], value_part[:, :tokens])
        count(2 * g + 1, key_part[:, tokens:], value_part[:, tokens:])
        return carry

    groups = inners // 2
    if groups <= 4:
        for g in range(1, groups):
            turn(g, 0)
    else:
        lax.fori_loop(1, groups, turn, 0)

    bias_own[...] = jnp.zeros((BIAS_ROWS, HEAD_DIM), F32)
    for g in range(GROUP):
        full = unrotate(dq_acc[g * tokens : (g + 1) * tokens] * SCALE)
        dq_ref[:, g * HEAD_DIM : (g + 1) * HEAD_DIM] = full.astype(BF16)
        bias_own[g : g + 1] = jnp.sum(full, axis=0, keepdims=True)
    stores[0].start()

    sums_t = jnp.transpose(sums[...])
    key_sums = sums_t[:inners]
    key_sums = key_sums * start_cos + pltpu.roll(key_sums, half, 1) * start_sin
    bias_own[GROUP : GROUP + 1] = jnp.sum(key_sums, axis=0, keepdims=True) * SCALE
    bias_own[GROUP + 1 : GROUP + 2] = jnp.sum(sums_t[half : half + inners], axis=0, keepdims=True)

    def bias_copy(step, slot):
        return pltpu.make_async_remote_copy(
            src_ref=bias_own,
            dst_ref=bias_in.at[slot],
            send_sem=bias_send.at[step],
            recv_sem=bias_recv.at[step],
            device_id=inner_id(step),
            device_id_type=MESH,
        )

    def plane_copy(step, slot):
        return pltpu.make_async_remote_copy(
            src_ref=plane_own,
            dst_ref=plane_in.at[slot],
            send_sem=plane_send.at[step],
            recv_sem=plane_recv.at[step],
            device_id=outer_id(step),
            device_id_type=MESH,
        )

    for step in range(1, inners):
        bias_copy(step, me).start()
    bias_in[me] = bias_own[...]
    for step in range(1, inners):
        bias_copy(step, partner(me, step, inners)).wait_recv()
    summed = bias_in[0]
    for slot in range(1, inners):
        summed = summed + bias_in[slot]
    plane_own[...] = summed
    for step in range(1, outers):
        plane_copy(step, plane).start()
    plane_in[plane] = summed

    total = own_acc[...]
    for step in range(1, inners):
        part_copy(step).wait_recv()
        total = total + part_in[step].astype(F32)
    key_full = unrotate(jnp.transpose(total[:HEAD_DIM]) * SCALE)
    value_full = jnp.transpose(total[HEAD_DIM:])
    dk_ref[...] = key_full.astype(BF16)
    dv_ref[...] = value_full.astype(BF16)
    stores[1].start()
    stores[2].start()

    for step in range(1, outers):
        plane_copy(step, partner(plane, step, outers)).wait_recv()
    for head in range(KV_HEADS):
        whole = plane_in[head]
        for other in range(head + KV_HEADS, outers, KV_HEADS):
            whole = whole + plane_in[other]
        bias_ref[head * GROUP : (head + 1) * GROUP] = whole[:GROUP]
        bias_ref[HEADS + head : HEADS + head + 1] = whole[GROUP : GROUP + 1]
        at = HEADS + KV_HEADS + head
        bias_ref[at : at + 1] = whole[GROUP + 1 : GROUP + 2]
    stores[3].start()

    for step in range(1, inners):
        kv_copy(step).wait_send()
        part_copy(step).wait_send()
        bias_copy(step, me).wait_send()
    for step in range(1, outers):
        plane_copy(step, plane).wait_send()
    for store in stores:
        store.wait()


def write(*refs):
    sources, targets, sem = refs[:4], refs[4:8], refs[8]
    copies = [
        pltpu.make_async_copy(source, target, sem.at[i])
        for i, (source, target) in enumerate(zip(sources, targets))
    ]
    for copy in copies:
        copy.start()
    for copy in copies:
        copy.wait()


def rotary(positions):
    frequency = np.exp(np.arange(HEAD_DIM // 2) * (-2.0 * math.log(ROPE_BASE) / HEAD_DIM))
    angles = np.asarray(positions)[:, None] * frequency[None, :]
    return np.concatenate([np.sin(angles), np.cos(angles)], axis=1).astype(np.float32)


def local(inners, outers, query_rot, key_rot, value_rows, attention_out, grad_out, log_norm,
          segments, block_table):
    del block_table
    tokens = query_rot.shape[1]
    rows = GROUP * tokens
    if segments.shape[0] > 1:
        example = lax.axis_index("outer") // KV_HEADS
        segments = lax.dynamic_slice_in_dim(segments, example, 1, 0)
    hbm = pl.BlockSpec(memory_space=pltpu.HBM)
    sems = pltpu.SemaphoreType.DMA
    shapes = (
        jax.ShapeDtypeStruct((tokens, GROUP * HEAD_DIM), BF16),
        jax.ShapeDtypeStruct((tokens, HEAD_DIM), BF16),
        jax.ShapeDtypeStruct((tokens, HEAD_DIM), BF16),
        jax.ShapeDtypeStruct((HEADS + 2 * KV_HEADS, HEAD_DIM), F32),
    )
    outs = pl.pallas_call(
        functools.partial(kernel, inners, outers),
        out_shape=shapes,
        in_specs=[hbm] * 9,
        out_specs=(hbm,) * 4,
        scratch_shapes=[
            pltpu.VMEM((tokens, HEAD_DIM), BF16),
            pltpu.VMEM((tokens, HEAD_DIM), BF16),
            pltpu.VMEM((1, tokens), jnp.int32),
            pltpu.VMEM((tokens, GROUP * HEAD_DIM), BF16),
            pltpu.VMEM((tokens, GROUP * HEAD_DIM), BF16),
            pltpu.VMEM((tokens, GROUP * HEAD_DIM), BF16),
            pltpu.VMEM((GROUP, 1, tokens), F32),
            pltpu.VMEM((tokens, HEAD_DIM), F32),
            pltpu.VMEM((inners, HEAD_DIM), F32),
            sems((9,)),
            pltpu.VMEM((tokens, GROUP * HEAD_DIM), BF16),
            pltpu.VMEM((tokens, HEAD_DIM), BF16),
            pltpu.VMEM((tokens, HEAD_DIM), BF16),
            pltpu.VMEM((HEADS + 2 * KV_HEADS, HEAD_DIM), F32),
            sems((4,)),
            pltpu.VMEM((inners, 3 * HEAD_DIM, tokens), BF16),
            pltpu.VMEM((rows, 2 * HEAD_DIM), BF16),
            pltpu.VMEM((rows, 2 * HEAD_DIM), BF16),
            pltpu.VMEM((HEAD_DIM, rows), BF16),
            pltpu.VMEM((HEAD_DIM, rows), BF16),
            pltpu.VMEM((rows, 2 * tokens), BF16),
            pltpu.VMEM((rows, 2 * tokens), BF16),
            pltpu.VMEM((rows, HEAD_DIM), F32),
            pltpu.VMEM((2 * HEAD_DIM, tokens), F32),
            pltpu.VMEM((inners, 2 * HEAD_DIM, tokens), BF16),
            pltpu.VMEM((inners, 2 * HEAD_DIM, tokens), BF16),
            pltpu.VMEM((HEAD_DIM, HEAD_DIM), F32),
            pltpu.VMEM((inners, HEAD_DIM), F32),
            pltpu.VMEM((BIAS_ROWS, HEAD_DIM), F32),
            pltpu.VMEM((inners, BIAS_ROWS, HEAD_DIM), F32),
            pltpu.VMEM((BIAS_ROWS, HEAD_DIM), F32),
            pltpu.VMEM((outers, BIAS_ROWS, HEAD_DIM), F32),
            sems((inners,)), sems((inners,)), sems((inners,)), sems((inners,)),
            sems((inners,)), sems((inners,)), sems((outers,)), sems((outers,)),
        ],
        compiler_params=pltpu.CompilerParams(
            collective_id=0, has_side_effects=True, vmem_limit_bytes=VMEM_LIMIT
        ),
        name="attention_backward",
    )(
        key_rot[0], value_rows[0], segments, query_rot[0], grad_out[0], attention_out[0],
        log_norm.reshape(GROUP, 1, tokens), jnp.asarray(rotary(np.arange(tokens))),
        jnp.asarray(rotary(np.arange(inners) * tokens)),
    )
    outs = pl.pallas_call(
        write,
        out_shape=shapes,
        in_specs=[hbm] * 4,
        out_specs=(hbm,) * 4,
        scratch_shapes=[sems((4,))],
        compiler_params=pltpu.CompilerParams(vmem_limit_bytes=VMEM_LIMIT),
        name="write_results",
    )(*outs)
    return outs[0][None], outs[1][None], outs[2][None], outs[3].reshape(-1)


def solution(mesh):
    placed = (
        P("outer", "inner", None),
        P("outer", "inner", None),
        P("outer", "inner", None),
        P("outer", "inner", None),
        P("outer", "inner", None),
        P("outer", None, "inner"),
        P(None, "inner"),
        P(None, "inner", None),
    )
    return jax.shard_map(
        functools.partial(local, mesh.shape["inner"], mesh.shape["outer"]),
        mesh=mesh,
        in_specs=placed,
        out_specs=(
            P("outer", "inner", None),
            P("outer", "inner", None),
            P("outer", "inner", None),
            P(),
        ),
        check_vma=False,
    )
```

```python
import functools
import math

import jax
import jax.numpy as jnp
import numpy as np
from jax import lax
from jax.experimental import pallas as pl
from jax.experimental.pallas import tpu as pltpu
from jax.sharding import PartitionSpec as P

HEADS = 28
KV_HEADS = 4
HEAD_DIM = 128
GROUP = HEADS // KV_HEADS
ROPE_BASE = 1000000.0
ROOT = math.sqrt(HEAD_DIM)
SCALE = 1.0 / ROOT
EXP2_SCALE = math.log2(math.e) / ROOT
MASKED = -1e30
EXTRA = 16
BIAS_ROWS = 16
VMEM_LIMIT = 63 * 1024 * 1024
MESH = pl.DeviceIdType.MESH
F32 = jnp.float32
BF16 = jnp.bfloat16


def partner(index, step, count):
    result = 0
    bit = 1
    while bit < count:
        result = result + ((index // bit + step // bit) % 2) * bit
        bit *= 2
    return result


def pieces(x):
    high = x.astype(BF16).astype(F32)
    rest = x - high
    middle = rest.astype(BF16).astype(F32)
    return high, middle, rest - middle


def dot(a, b):
    return jnp.dot(a, b, preferred_element_type=F32)


def kernel(
    inners, outers, k_hbm, v_hbm, seg_hbm, q_hbm, go_hbm, ao_hbm, norm_hbm, base_hbm, starts_hbm,
    dq_hbm, dk_hbm, dv_hbm, bias_hbm,
    k_ref, v_ref, seg_ref, q_ref, go_ref, ao_ref, norm_ref, base_ref, starts_ref, load_sem,
    dq_ref, dk_ref, dv_ref, bias_ref, store_sem,
    kv, q_aug, go_aug, q_t, go_t, probs, grads, dq_acc, own_acc, kept, pair_out, pair_in,
    part_out, part_in,
    sums, angles, bias_own, bias_in, plane_own, plane_in,
    kv_send, kv_recv, pair_send, pair_recv, part_send, part_recv, bias_send, bias_recv, plane_send, plane_recv,
):
    tokens = k_ref.shape[0]
    rows = GROUP * tokens
    me = lax.axis_index("inner")
    plane = lax.axis_index("outer")

    loads = [
        pltpu.make_async_copy(source, target, load_sem.at[i])
        for i, (source, target) in enumerate([
            (k_hbm, k_ref), (v_hbm, v_ref), (seg_hbm, seg_ref), (q_hbm, q_ref), (go_hbm, go_ref),
            (ao_hbm, ao_ref), (norm_hbm, norm_ref), (base_hbm, base_ref), (starts_hbm, starts_ref),
        ])
    ]
    for load in loads:
        load.start()
    stores = [
        pltpu.make_async_copy(source, target, store_sem.at[i])
        for i, (source, target) in enumerate([
            (dq_ref, dq_hbm), (dk_ref, dk_hbm), (dv_ref, dv_hbm), (bias_ref, bias_hbm),
        ])
    ]

    def inner_id(step):
        return (plane, partner(me, step, inners))

    def outer_id(step):
        return (partner(plane, step, outers), me)

    barrier = pltpu.get_barrier_semaphore()
    for step in range(1, inners):
        pl.semaphore_signal(barrier, inc=1, device_id=inner_id(step), device_id_type=MESH)
    for step in range(1, outers):
        pl.semaphore_signal(barrier, inc=1, device_id=outer_id(step), device_id_type=MESH)

    for load in loads[:3]:
        load.wait()
    seg = seg_ref[...].astype(F32)
    row = lax.broadcasted_iota(jnp.int32, (EXTRA, tokens), 0)
    seg_rows = jnp.broadcast_to(seg, (EXTRA, tokens))
    extra = jnp.where(row < 3, 1.0, 0.0)
    extra = jnp.where((row == 3) & (seg_rows == 1.0), 1.0, extra)
    extra = jnp.where((row == 4) & (seg_rows == 2.0), 1.0, extra)
    kv[0, :HEAD_DIM] = jnp.transpose(v_ref[...])
    kv[0, HEAD_DIM : 2 * HEAD_DIM] = jnp.transpose(k_ref[...])
    kv[0, 2 * HEAD_DIM : 2 * HEAD_DIM + EXTRA] = extra.astype(BF16)
    for slot in range(inners):
        kv[slot, 2 * HEAD_DIM + EXTRA :] = jnp.zeros((HEAD_DIM - EXTRA, tokens), BF16)

    pl.semaphore_wait(barrier, inners + outers - 2)

    sent = 2 * HEAD_DIM + EXTRA

    def kv_copy(step):
        return pltpu.make_async_remote_copy(
            src_ref=kv.at[0, pl.ds(0, sent)],
            dst_ref=kv.at[step, pl.ds(0, sent)],
            send_sem=kv_send.at[step],
            recv_sem=kv_recv.at[step],
            device_id=inner_id(step),
            device_id_type=MESH,
        )

    def forward(step):
        return pltpu.make_async_remote_copy(
            src_ref=kv.at[step, pl.ds(0, sent)],
            dst_ref=kv.at[step + 1, pl.ds(0, sent)],
            send_sem=kv_send.at[step + 1],
            recv_sem=kv_recv.at[step + 1],
            device_id=inner_id(1),
            device_id_type=MESH,
        )

    def pair_copy(g):
        return pltpu.make_async_remote_copy(
            src_ref=pair_out.at[g],
            dst_ref=pair_in.at[g],
            send_sem=pair_send.at[g],
            recv_sem=pair_recv.at[g],
            device_id=inner_id(1),
            device_id_type=MESH,
        )

    def part_copy(step):
        return pltpu.make_async_remote_copy(
            src_ref=part_out.at[step],
            dst_ref=part_in.at[step],
            send_sem=part_send.at[step],
            recv_sem=part_recv.at[step],
            device_id=inner_id(step),
            device_id_type=MESH,
        )

    groups = inners // 2
    order = [1, 3, 2] if groups == 4 else list(range(1, groups))
    direct = [1] + [2 * g for g in range(1, groups)]
    for step in direct:
        kv_copy(step).start()

    for load in loads[3:]:
        load.wait()
    row8 = lax.broadcasted_iota(jnp.int32, (8, tokens), 0)
    seg8 = jnp.broadcast_to(seg, (8, tokens))
    masks = jnp.where((row8 == 3) & (seg8 != 1.0), MASKED, 0.0)
    masks = jnp.where((row8 == 4) & (seg8 != 2.0), MASKED, masks)
    lane = lax.broadcasted_iota(jnp.int32, (tokens, HEAD_DIM), 1)
    for g in range(GROUP):
        here = slice(g * tokens, (g + 1) * tokens)
        cols = slice(g * HEAD_DIM, (g + 1) * HEAD_DIM)
        query = q_ref[:, cols]
        grad = go_ref[:, cols]
        q_aug[here, :HEAD_DIM] = query
        go_aug[here, :HEAD_DIM] = grad
        q_t[:, here] = jnp.transpose(query)
        go_t[:, here] = jnp.transpose(grad)
        high, middle, low = pieces(norm_ref[g] * -ROOT)
        top = jnp.where(row8 == 0, high, masks)
        top = jnp.where(row8 == 1, middle, top)
        top = jnp.where(row8 == 2, low, top)
        full = jnp.concatenate([top, jnp.zeros((HEAD_DIM - 8, tokens), F32)], axis=0)
        q_aug[here, HEAD_DIM:] = jnp.transpose(full).astype(BF16)
        delta = -jnp.sum(
            grad.astype(F32) * ao_ref[:, cols].astype(F32), axis=1, keepdims=True
        )
        d_high, d_middle, d_low = pieces(delta)
        side = jnp.where(lane == 0, d_high, 0.0)
        side = jnp.where(lane == 1, d_middle, side)
        side = jnp.where(lane == 2, d_low, side)
        go_aug[here, HEAD_DIM:] = side.astype(BF16)

    half = HEAD_DIM // 2
    for slot in range(inners):
        angles[slot : slot + 1] = starts_ref[pl.ds(partner(me, slot, inners), 1)]

    def both(table):
        below = lax.broadcasted_iota(jnp.int32, table.shape, 1) < half
        turned = pltpu.roll(table, half, 1)
        return jnp.where(below, turned, table), jnp.where(below, table, -turned)

    base_cos, base_sin = both(base_ref[...])
    start_cos, start_sin = both(angles[...])
    cosine = base_cos * start_cos[:1] - base_sin * start_sin[:1]
    sine = base_sin * start_cos[:1] + base_cos * start_sin[:1]
    base_t = jnp.transpose(base_ref[...])
    sine_t, cosine_t = base_t[:half], base_t[half:]
    sums[...] = jnp.zeros((HEAD_DIM, HEAD_DIM), F32)
    sum_lane = lax.broadcasted_iota(jnp.int32, (HEAD_DIM, HEAD_DIM), 1)

    def unrotate(x):
        return x * cosine + pltpu.roll(x, half, 1) * sine

    chunk = 256
    starts = list(range(0, rows, chunk))

    def compute(g, first):
        block = jnp.concatenate([kv[2 * g], kv[2 * g + 1]], axis=1)
        values_t = jnp.concatenate([block[:HEAD_DIM], block[2 * HEAD_DIM :]], axis=0)
        keys_t = block[HEAD_DIM:]
        keys = jnp.transpose(block[HEAD_DIM : 2 * HEAD_DIM])
        for start in starts:
            here = slice(start, min(start + chunk, rows))
            scores = dot(q_aug[here], keys_t)
            chances = jnp.exp2(scores * EXP2_SCALE)
            probs[here] = chances.astype(BF16)
            low_grads = (chances * dot(go_aug[here], values_t)).astype(BF16)
            grads[here] = low_grads
            part = dot(low_grads, keys)
            if first:
                dq_acc[here] = part
            else:
                dq_acc[here] += part
        value_part = dot(go_t[...], probs[...])
        key_part = dot(q_t[...], grads[...])
        return key_part, value_part

    def count(slot, key_part, value_part):
        upper, lower = key_part[:half], key_part[half:]
        key_sum = jnp.concatenate(
            [
                jnp.sum(upper * cosine_t + lower * sine_t, axis=1, keepdims=True),
                jnp.sum(lower * cosine_t - upper * sine_t, axis=1, keepdims=True),
            ],
            axis=0,
        )
        value_sum = jnp.sum(value_part, axis=1, keepdims=True)
        held = jnp.where(sum_lane == slot, key_sum, sums[...])
        sums[...] = jnp.where(sum_lane == half + slot, value_sum, held)

    def pass_on(g):
        kv_copy(2 * g).wait_recv()
        forward(2 * g).start()

    def turn(g):
        forward(2 * g).wait_recv()
        key_part, value_part = compute(g, False)
        pair_out[g, :HEAD_DIM] = key_part[:, tokens:].astype(BF16)
        pair_out[g, HEAD_DIM:] = value_part[:, tokens:].astype(BF16)
        pair_copy(g).start()
        kept[g, :HEAD_DIM] = key_part[:, :tokens]
        kept[g, HEAD_DIM:] = value_part[:, :tokens]
        count(2 * g, key_part[:, :tokens], value_part[:, :tokens])
        count(2 * g + 1, key_part[:, tokens:], value_part[:, tokens:])

    def send_home(g):
        pair_copy(g).wait_recv()
        part_out[2 * g] = (kept[g] + pair_in[g].astype(F32)).astype(BF16)
        part_copy(2 * g).start()

    kv_copy(1).wait_recv()
    key_part, value_part = compute(0, True)
    part_out[1, :HEAD_DIM] = key_part[:, tokens:].astype(BF16)
    part_out[1, HEAD_DIM:] = value_part[:, tokens:].astype(BF16)
    part_copy(1).start()
    own_acc[:HEAD_DIM] = key_part[:, :tokens]
    own_acc[HEAD_DIM:] = value_part[:, :tokens]
    count(0, key_part[:, :tokens], value_part[:, :tokens])
    count(1, key_part[:, tokens:], value_part[:, tokens:])
    if groups <= 4:
        for i, g in enumerate(order):
            if i == 0:
                pass_on(g)
            if i + 1 < len(order):
                pass_on(order[i + 1])
            turn(g)
            if i > 0:
                send_home(order[i - 1])
    else:

        def whole_turn(g, carry):
            pass_on(g)
            turn(g)
            send_home(g)
            return carry

        lax.fori_loop(1, groups, whole_turn, 0)

    bias_own[...] = jnp.zeros((BIAS_ROWS, HEAD_DIM), F32)
    for g in range(GROUP):
        full = unrotate(dq_acc[g * tokens : (g + 1) * tokens] * SCALE)
        dq_ref[:, g * HEAD_DIM : (g + 1) * HEAD_DIM] = full.astype(BF16)
        bias_own[g : g + 1] = jnp.sum(full, axis=0, keepdims=True)
    stores[0].start()

    if groups <= 4:
        send_home(order[-1])
    sums_t = jnp.transpose(sums[...])
    key_sums = sums_t[:inners]
    key_sums = key_sums * start_cos + pltpu.roll(key_sums, half, 1) * start_sin
    bias_own[GROUP : GROUP + 1] = jnp.sum(key_sums, axis=0, keepdims=True) * SCALE
    bias_own[GROUP + 1 : GROUP + 2] = jnp.sum(sums_t[half : half + inners], axis=0, keepdims=True)

    def bias_copy(step, slot):
        return pltpu.make_async_remote_copy(
            src_ref=bias_own,
            dst_ref=bias_in.at[slot],
            send_sem=bias_send.at[step],
            recv_sem=bias_recv.at[step],
            device_id=inner_id(step),
            device_id_type=MESH,
        )

    def plane_copy(step, slot):
        return pltpu.make_async_remote_copy(
            src_ref=plane_own,
            dst_ref=plane_in.at[slot],
            send_sem=plane_send.at[step],
            recv_sem=plane_recv.at[step],
            device_id=outer_id(step),
            device_id_type=MESH,
        )

    for step in range(1, inners):
        bias_copy(step, me).start()
    bias_in[me] = bias_own[...]
    for step in range(1, inners):
        bias_copy(step, partner(me, step, inners)).wait_recv()
    summed = bias_in[0]
    for slot in range(1, inners):
        summed = summed + bias_in[slot]
    plane_own[...] = summed
    for step in range(1, outers):
        plane_copy(step, plane).start()
    plane_in[plane] = summed

    total = own_acc[...]
    for step in direct:
        part_copy(step).wait_recv()
        total = total + part_in[step].astype(F32)
    key_full = unrotate(jnp.transpose(total[:HEAD_DIM]) * SCALE)
    value_full = jnp.transpose(total[HEAD_DIM:])
    dk_ref[...] = key_full.astype(BF16)
    dv_ref[...] = value_full.astype(BF16)
    stores[1].start()
    stores[2].start()

    for step in range(1, outers):
        plane_copy(step, partner(plane, step, outers)).wait_recv()
    for head in range(KV_HEADS):
        whole = plane_in[head]
        for other in range(head + KV_HEADS, outers, KV_HEADS):
            whole = whole + plane_in[other]
        bias_ref[head * GROUP : (head + 1) * GROUP] = whole[:GROUP]
        bias_ref[HEADS + head : HEADS + head + 1] = whole[GROUP : GROUP + 1]
        at = HEADS + KV_HEADS + head
        bias_ref[at : at + 1] = whole[GROUP + 1 : GROUP + 2]
    stores[3].start()

    for step in direct:
        kv_copy(step).wait_send()
        part_copy(step).wait_send()
    for g in range(1, groups):
        forward(2 * g).wait_send()
        pair_copy(g).wait_send()
    for step in range(1, inners):
        bias_copy(step, me).wait_send()
    for step in range(1, outers):
        plane_copy(step, plane).wait_send()
    for store in stores:
        store.wait()


def write(*refs):
    sources, targets, held, sem = refs[:4], refs[4:8], refs[8:12], refs[12]
    loads = [pltpu.make_async_copy(sources[i], held[i], sem.at[i]) for i in range(4)]
    stores = [pltpu.make_async_copy(held[i], targets[i], sem.at[4 + i]) for i in range(4)]
    for load in loads:
        load.start()
    for load, store in zip(loads, stores):
        load.wait()
        store.start()
    for store in stores:
        store.wait()


def rotary(positions):
    frequency = np.exp(np.arange(HEAD_DIM // 2) * (-2.0 * math.log(ROPE_BASE) / HEAD_DIM))
    angles = np.asarray(positions)[:, None] * frequency[None, :]
    return np.concatenate([np.sin(angles), np.cos(angles)], axis=1).astype(np.float32)


def local(inners, outers, query_rot, key_rot, value_rows, attention_out, grad_out, log_norm,
          segments, block_table):
    del block_table
    tokens = query_rot.shape[1]
    rows = GROUP * tokens
    if segments.shape[0] > 1:
        example = lax.axis_index("outer") // KV_HEADS
        segments = lax.dynamic_slice_in_dim(segments, example, 1, 0)
    hbm = pl.BlockSpec(memory_space=pltpu.HBM)
    sems = pltpu.SemaphoreType.DMA
    shapes = (
        jax.ShapeDtypeStruct((tokens, GROUP * HEAD_DIM), BF16),
        jax.ShapeDtypeStruct((tokens, HEAD_DIM), BF16),
        jax.ShapeDtypeStruct((tokens, HEAD_DIM), BF16),
        jax.ShapeDtypeStruct((HEADS + 2 * KV_HEADS, HEAD_DIM), F32),
    )
    outs = pl.pallas_call(
        functools.partial(kernel, inners, outers),
        out_shape=shapes,
        in_specs=[hbm] * 9,
        out_specs=(hbm,) * 4,
        scratch_shapes=[
            pltpu.VMEM((tokens, HEAD_DIM), BF16),
            pltpu.VMEM((tokens, HEAD_DIM), BF16),
            pltpu.VMEM((1, tokens), jnp.int32),
            pltpu.VMEM((tokens, GROUP * HEAD_DIM), BF16),
            pltpu.VMEM((tokens, GROUP * HEAD_DIM), BF16),
            pltpu.VMEM((tokens, GROUP * HEAD_DIM), BF16),
            pltpu.VMEM((GROUP, 1, tokens), F32),
            pltpu.VMEM((tokens, HEAD_DIM), F32),
            pltpu.VMEM((inners, HEAD_DIM), F32),
            sems((9,)),
            pltpu.VMEM((tokens, GROUP * HEAD_DIM), BF16),
            pltpu.VMEM((tokens, HEAD_DIM), BF16),
            pltpu.VMEM((tokens, HEAD_DIM), BF16),
            pltpu.VMEM((HEADS + 2 * KV_HEADS, HEAD_DIM), F32),
            sems((4,)),
            pltpu.VMEM((inners, 3 * HEAD_DIM, tokens), BF16),
            pltpu.VMEM((rows, 2 * HEAD_DIM), BF16),
            pltpu.VMEM((rows, 2 * HEAD_DIM), BF16),
            pltpu.VMEM((HEAD_DIM, rows), BF16),
            pltpu.VMEM((HEAD_DIM, rows), BF16),
            pltpu.VMEM((rows, 2 * tokens), BF16),
            pltpu.VMEM((rows, 2 * tokens), BF16),
            pltpu.VMEM((rows, HEAD_DIM), F32),
            pltpu.VMEM((2 * HEAD_DIM, tokens), F32),
            pltpu.VMEM((inners // 2, 2 * HEAD_DIM, tokens), F32),
            pltpu.VMEM((inners // 2, 2 * HEAD_DIM, tokens), BF16),
            pltpu.VMEM((inners // 2, 2 * HEAD_DIM, tokens), BF16),
            pltpu.VMEM((inners, 2 * HEAD_DIM, tokens), BF16),
            pltpu.VMEM((inners, 2 * HEAD_DIM, tokens), BF16),
            pltpu.VMEM((HEAD_DIM, HEAD_DIM), F32),
            pltpu.VMEM((inners, HEAD_DIM), F32),
            pltpu.VMEM((BIAS_ROWS, HEAD_DIM), F32),
            pltpu.VMEM((inners, BIAS_ROWS, HEAD_DIM), F32),
            pltpu.VMEM((BIAS_ROWS, HEAD_DIM), F32),
            pltpu.VMEM((outers, BIAS_ROWS, HEAD_DIM), F32),
            sems((inners,)), sems((inners,)), sems((inners // 2,)), sems((inners // 2,)),
            sems((inners,)), sems((inners,)),
            sems((inners,)), sems((inners,)), sems((outers,)), sems((outers,)),
        ],
        compiler_params=pltpu.CompilerParams(
            collective_id=0, has_side_effects=True, vmem_limit_bytes=VMEM_LIMIT
        ),
        name="attention_backward",
    )(
        key_rot[0], value_rows[0], segments, query_rot[0], grad_out[0], attention_out[0],
        log_norm.reshape(GROUP, 1, tokens), jnp.asarray(rotary(np.arange(tokens))),
        jnp.asarray(rotary(np.arange(inners) * tokens)),
    )
    outs = pl.pallas_call(
        write,
        out_shape=shapes,
        in_specs=[hbm] * 4,
        out_specs=(hbm,) * 4,
        scratch_shapes=[pltpu.VMEM(shape.shape, shape.dtype) for shape in shapes] + [sems((8,))],
        compiler_params=pltpu.CompilerParams(vmem_limit_bytes=VMEM_LIMIT),
        name="write_results",
    )(*outs)
    return outs[0][None], outs[1][None], outs[2][None], outs[3].reshape(-1)


def solution(mesh):
    placed = (
        P("outer", "inner", None),
        P("outer", "inner", None),
        P("outer", "inner", None),
        P("outer", "inner", None),
        P("outer", "inner", None),
        P("outer", None, "inner"),
        P(None, "inner"),
        P(None, "inner", None),
    )
    return jax.shard_map(
        functools.partial(local, mesh.shape["inner"], mesh.shape["outer"]),
        mesh=mesh,
        in_specs=placed,
        out_specs=(
            P("outer", "inner", None),
            P("outer", "inner", None),
            P("outer", "inner", None),
            P(),
        ),
        check_vma=False,
    )
```

```python
import functools
import math

import jax
import jax.numpy as jnp
import numpy as np
from jax import lax
from jax.experimental import pallas as pl
from jax.experimental.pallas import tpu as pltpu
from jax.sharding import PartitionSpec as P

HEADS = 28
KV_HEADS = 4
HEAD_DIM = 128
GROUP = HEADS // KV_HEADS
ROPE_BASE = 1000000.0
ROOT = math.sqrt(HEAD_DIM)
SCALE = 1.0 / ROOT
MASKED = -1e30
EXTRA = 16
BIAS_ROWS = 16
VMEM_LIMIT = 63 * 1024 * 1024
MESH = pl.DeviceIdType.MESH
F32 = jnp.float32
BF16 = jnp.bfloat16


def partner(index, step, count):
    result = 0
    bit = 1
    while bit < count:
        result = result + ((index // bit + step // bit) % 2) * bit
        bit *= 2
    return result


def pieces(x):
    high = x.astype(BF16).astype(F32)
    rest = x - high
    middle = rest.astype(BF16).astype(F32)
    return high, middle, rest - middle


def dot(a, b):
    return jnp.dot(a, b, preferred_element_type=F32)


def kernel(
    inners, outers, k_hbm, v_hbm, seg_hbm, q_hbm, go_hbm, ao_hbm, norm_hbm, base_hbm, starts_hbm,
    dq_hbm, dk_hbm, dv_hbm, bias_hbm,
    k_ref, v_ref, seg_ref, q_ref, go_ref, ao_ref, norm_ref, base_ref, starts_ref, load_sem,
    dq_ref, dk_ref, dv_ref, bias_ref, store_sem,
    kv, q_aug, go_aug, q_t, go_t, probs, grads, dq_acc, own_acc, kept, pair_out, pair_in,
    part_out, part_in,
    sums, angles, bias_own, bias_in, plane_own, plane_in,
    kv_send, kv_recv, pair_send, pair_recv, part_send, part_recv, bias_send, bias_recv, plane_send, plane_recv,
):
    tokens = k_ref.shape[0]
    rows = GROUP * tokens
    me = lax.axis_index("inner")
    plane = lax.axis_index("outer")

    loads = [
        pltpu.make_async_copy(source, target, load_sem.at[i])
        for i, (source, target) in enumerate([
            (k_hbm, k_ref), (v_hbm, v_ref), (seg_hbm, seg_ref), (q_hbm, q_ref), (go_hbm, go_ref),
            (ao_hbm, ao_ref), (norm_hbm, norm_ref), (base_hbm, base_ref), (starts_hbm, starts_ref),
        ])
    ]
    for load in loads:
        load.start()
    stores = [
        pltpu.make_async_copy(source, target, store_sem.at[i])
        for i, (source, target) in enumerate([
            (dq_ref, dq_hbm), (dk_ref, dk_hbm), (dv_ref, dv_hbm), (bias_ref, bias_hbm),
        ])
    ]

    def inner_id(step):
        return (plane, partner(me, step, inners))

    def outer_id(step):
        return (partner(plane, step, outers), me)

    barrier = pltpu.get_barrier_semaphore()
    for step in range(1, inners):
        pl.semaphore_signal(barrier, inc=1, device_id=inner_id(step), device_id_type=MESH)
    for step in range(1, outers):
        pl.semaphore_signal(barrier, inc=1, device_id=outer_id(step), device_id_type=MESH)

    for load in loads[:3]:
        load.wait()
    seg = seg_ref[...].astype(F32)
    row = lax.broadcasted_iota(jnp.int32, (EXTRA, tokens), 0)
    seg_rows = jnp.broadcast_to(seg, (EXTRA, tokens))
    extra = jnp.where(row < 3, 1.0, 0.0)
    extra = jnp.where((row == 3) & (seg_rows == 1.0), 1.0, extra)
    extra = jnp.where((row == 4) & (seg_rows == 2.0), 1.0, extra)
    kv[0, :HEAD_DIM] = jnp.transpose(v_ref[...])
    kv[0, HEAD_DIM : 2 * HEAD_DIM] = jnp.transpose(k_ref[...])
    kv[0, 2 * HEAD_DIM : 2 * HEAD_DIM + EXTRA] = extra.astype(BF16)
    for slot in range(inners):
        kv[slot, 2 * HEAD_DIM + EXTRA :] = jnp.zeros((HEAD_DIM - EXTRA, tokens), BF16)

    pl.semaphore_wait(barrier, inners + outers - 2)

    sent = 2 * HEAD_DIM + EXTRA

    def kv_copy(step):
        return pltpu.make_async_remote_copy(
            src_ref=kv.at[0, pl.ds(0, sent)],
            dst_ref=kv.at[step, pl.ds(0, sent)],
            send_sem=kv_send.at[step],
            recv_sem=kv_recv.at[step],
            device_id=inner_id(step),
            device_id_type=MESH,
        )

    def forward(step):
        return pltpu.make_async_remote_copy(
            src_ref=kv.at[step, pl.ds(0, sent)],
            dst_ref=kv.at[step + 1, pl.ds(0, sent)],
            send_sem=kv_send.at[step + 1],
            recv_sem=kv_recv.at[step + 1],
            device_id=inner_id(1),
            device_id_type=MESH,
        )

    def pair_copy(g):
        return pltpu.make_async_remote_copy(
            src_ref=pair_out.at[g],
            dst_ref=pair_in.at[g],
            send_sem=pair_send.at[g],
            recv_sem=pair_recv.at[g],
            device_id=inner_id(1),
            device_id_type=MESH,
        )

    def part_copy(step):
        return pltpu.make_async_remote_copy(
            src_ref=part_out.at[step],
            dst_ref=part_in.at[step],
            send_sem=part_send.at[step],
            recv_sem=part_recv.at[step],
            device_id=inner_id(step),
            device_id_type=MESH,
        )

    groups = inners // 2
    order = [1, 3, 2] if groups == 4 else list(range(1, groups))
    direct = [1] + [2 * g for g in range(1, groups)]
    for step in direct:
        kv_copy(step).start()

    for load in loads[3:]:
        load.wait()
    row8 = lax.broadcasted_iota(jnp.int32, (8, tokens), 0)
    seg8 = jnp.broadcast_to(seg, (8, tokens))
    masks = jnp.where((row8 == 3) & (seg8 != 1.0), MASKED, 0.0)
    masks = jnp.where((row8 == 4) & (seg8 != 2.0), MASKED, masks)
    lane = lax.broadcasted_iota(jnp.int32, (tokens, HEAD_DIM), 1)
    for g in range(GROUP):
        here = slice(g * tokens, (g + 1) * tokens)
        cols = slice(g * HEAD_DIM, (g + 1) * HEAD_DIM)
        query = q_ref[:, cols]
        grad = go_ref[:, cols]
        q_aug[here, :HEAD_DIM] = query
        go_aug[here, :HEAD_DIM] = grad
        q_t[:, here] = jnp.transpose(query)
        go_t[:, here] = jnp.transpose(grad)
        high, middle, low = pieces(norm_ref[g] * -ROOT)
        top = jnp.where(row8 == 0, high, masks)
        top = jnp.where(row8 == 1, middle, top)
        top = jnp.where(row8 == 2, low, top)
        full = jnp.concatenate([top, jnp.zeros((HEAD_DIM - 8, tokens), F32)], axis=0)
        q_aug[here, HEAD_DIM:] = jnp.transpose(full).astype(BF16)
        delta = -jnp.sum(
            grad.astype(F32) * ao_ref[:, cols].astype(F32), axis=1, keepdims=True
        )
        d_high, d_middle, d_low = pieces(delta)
        side = jnp.where(lane == 0, d_high, 0.0)
        side = jnp.where(lane == 1, d_middle, side)
        side = jnp.where(lane == 2, d_low, side)
        go_aug[here, HEAD_DIM:] = side.astype(BF16)

    half = HEAD_DIM // 2
    for slot in range(inners):
        angles[slot : slot + 1] = starts_ref[pl.ds(partner(me, slot, inners), 1)]

    def both(table):
        below = lax.broadcasted_iota(jnp.int32, table.shape, 1) < half
        turned = pltpu.roll(table, half, 1)
        return jnp.where(below, turned, table), jnp.where(below, table, -turned)

    base_cos, base_sin = both(base_ref[...])
    start_cos, start_sin = both(angles[...])
    cosine = base_cos * start_cos[:1] - base_sin * start_sin[:1]
    sine = base_sin * start_cos[:1] + base_cos * start_sin[:1]
    base_t = jnp.transpose(base_ref[...])
    sine_t, cosine_t = base_t[:half], base_t[half:]
    sums[...] = jnp.zeros((HEAD_DIM, HEAD_DIM), F32)
    sum_lane = lax.broadcasted_iota(jnp.int32, (HEAD_DIM, HEAD_DIM), 1)

    def unrotate(x):
        return x * cosine + pltpu.roll(x, half, 1) * sine

    chunk = rows if tokens <= 128 else 256
    starts = list(range(0, rows, chunk))

    def compute(g, first):
        block = jnp.concatenate([kv[2 * g], kv[2 * g + 1]], axis=1)
        values_t = jnp.concatenate([block[:HEAD_DIM], block[2 * HEAD_DIM :]], axis=0)
        keys_t = block[HEAD_DIM:]
        keys = jnp.transpose(block[HEAD_DIM : 2 * HEAD_DIM])
        for start in starts:
            here = slice(start, min(start + chunk, rows))
            scores = dot(q_aug[here], keys_t)
            chances = jnp.exp(scores * SCALE)
            probs[here] = chances.astype(BF16)
            low_grads = (chances * dot(go_aug[here], values_t)).astype(BF16)
            grads[here] = low_grads
            part = dot(low_grads, keys)
            if first:
                dq_acc[here] = part
            else:
                dq_acc[here] += part
        value_part = dot(go_t[...], probs[...])
        key_part = dot(q_t[...], grads[...])
        return key_part, value_part

    def count(slot, key_part, value_part):
        upper, lower = key_part[:half], key_part[half:]
        key_sum = jnp.concatenate(
            [
                jnp.sum(upper * cosine_t + lower * sine_t, axis=1, keepdims=True),
                jnp.sum(lower * cosine_t - upper * sine_t, axis=1, keepdims=True),
            ],
            axis=0,
        )
        value_sum = jnp.sum(value_part, axis=1, keepdims=True)
        held = jnp.where(sum_lane == slot, key_sum, sums[...])
        sums[...] = jnp.where(sum_lane == half + slot, value_sum, held)

    def pass_on(g):
        kv_copy(2 * g).wait_recv()
        forward(2 * g).start()

    def turn(g):
        forward(2 * g).wait_recv()
        key_part, value_part = compute(g, False)
        pair_out[g, :HEAD_DIM] = key_part[:, tokens:].astype(BF16)
        pair_out[g, HEAD_DIM:] = value_part[:, tokens:].astype(BF16)
        pair_copy(g).start()
        kept[g, :HEAD_DIM] = key_part[:, :tokens]
        kept[g, HEAD_DIM:] = value_part[:, :tokens]
        count(2 * g, key_part[:, :tokens], value_part[:, :tokens])
        count(2 * g + 1, key_part[:, tokens:], value_part[:, tokens:])

    def send_home(g):
        pair_copy(g).wait_recv()
        part_out[2 * g] = (kept[g] + pair_in[g].astype(F32)).astype(BF16)
        part_copy(2 * g).start()

    kv_copy(1).wait_recv()
    key_part, value_part = compute(0, True)
    part_out[1, :HEAD_DIM] = key_part[:, tokens:].astype(BF16)
    part_out[1, HEAD_DIM:] = value_part[:, tokens:].astype(BF16)
    part_copy(1).start()
    own_acc[:HEAD_DIM] = key_part[:, :tokens]
    own_acc[HEAD_DIM:] = value_part[:, :tokens]
    count(0, key_part[:, :tokens], value_part[:, :tokens])
    count(1, key_part[:, tokens:], value_part[:, tokens:])
    if groups <= 4:
        for i, g in enumerate(order):
            if i == 0:
                pass_on(g)
            if i + 1 < len(order):
                pass_on(order[i + 1])
            turn(g)
            if i > 0:
                send_home(order[i - 1])
    else:

        def whole_turn(g, carry):
            pass_on(g)
            turn(g)
            send_home(g)
            return carry

        lax.fori_loop(1, groups, whole_turn, 0)

    bias_own[...] = jnp.zeros((BIAS_ROWS, HEAD_DIM), F32)
    for g in range(GROUP):
        full = unrotate(dq_acc[g * tokens : (g + 1) * tokens] * SCALE)
        dq_ref[:, g * HEAD_DIM : (g + 1) * HEAD_DIM] = full.astype(BF16)
        bias_own[g : g + 1] = jnp.sum(full, axis=0, keepdims=True)
    stores[0].start()

    if groups <= 4:
        send_home(order[-1])
    sums_t = jnp.transpose(sums[...])
    key_sums = sums_t[:inners]
    key_sums = key_sums * start_cos + pltpu.roll(key_sums, half, 1) * start_sin
    bias_own[GROUP : GROUP + 1] = jnp.sum(key_sums, axis=0, keepdims=True) * SCALE
    bias_own[GROUP + 1 : GROUP + 2] = jnp.sum(sums_t[half : half + inners], axis=0, keepdims=True)

    def bias_copy(step, slot):
        return pltpu.make_async_remote_copy(
            src_ref=bias_own,
            dst_ref=bias_in.at[slot],
            send_sem=bias_send.at[step],
            recv_sem=bias_recv.at[step],
            device_id=inner_id(step),
            device_id_type=MESH,
        )

    def plane_copy(step, slot):
        return pltpu.make_async_remote_copy(
            src_ref=plane_own,
            dst_ref=plane_in.at[slot],
            send_sem=plane_send.at[step],
            recv_sem=plane_recv.at[step],
            device_id=outer_id(step),
            device_id_type=MESH,
        )

    for step in range(1, inners):
        bias_copy(step, me).start()
    bias_in[me] = bias_own[...]
    for step in range(1, inners):
        bias_copy(step, partner(me, step, inners)).wait_recv()
    summed = bias_in[0]
    for slot in range(1, inners):
        summed = summed + bias_in[slot]
    plane_own[...] = summed
    for step in range(1, outers):
        plane_copy(step, plane).start()
    plane_in[plane] = summed

    total = own_acc[...]
    for step in direct:
        part_copy(step).wait_recv()
        total = total + part_in[step].astype(F32)
    key_full = unrotate(jnp.transpose(total[:HEAD_DIM]) * SCALE)
    value_full = jnp.transpose(total[HEAD_DIM:])
    dk_ref[...] = key_full.astype(BF16)
    dv_ref[...] = value_full.astype(BF16)
    stores[1].start()
    stores[2].start()

    for step in range(1, outers):
        plane_copy(step, partner(plane, step, outers)).wait_recv()
    for head in range(KV_HEADS):
        whole = plane_in[head]
        for other in range(head + KV_HEADS, outers, KV_HEADS):
            whole = whole + plane_in[other]
        bias_ref[head * GROUP : (head + 1) * GROUP] = whole[:GROUP]
        bias_ref[HEADS + head : HEADS + head + 1] = whole[GROUP : GROUP + 1]
        at = HEADS + KV_HEADS + head
        bias_ref[at : at + 1] = whole[GROUP + 1 : GROUP + 2]
    stores[3].start()

    for step in direct:
        kv_copy(step).wait_send()
        part_copy(step).wait_send()
    for g in range(1, groups):
        forward(2 * g).wait_send()
        pair_copy(g).wait_send()
    for step in range(1, inners):
        bias_copy(step, me).wait_send()
    for step in range(1, outers):
        plane_copy(step, plane).wait_send()
    for store in stores:
        store.wait()


def write(*refs):
    sources, targets, held, sem = refs[:4], refs[4:8], refs[8:12], refs[12]
    loads = [pltpu.make_async_copy(sources[i], held[i], sem.at[i]) for i in range(4)]
    stores = [pltpu.make_async_copy(held[i], targets[i], sem.at[4 + i]) for i in range(4)]
    for load in loads:
        load.start()
    for load, store in zip(loads, stores):
        load.wait()
        store.start()
    for store in stores:
        store.wait()


def rotary(positions):
    frequency = np.exp(np.arange(HEAD_DIM // 2) * (-2.0 * math.log(ROPE_BASE) / HEAD_DIM))
    angles = np.asarray(positions)[:, None] * frequency[None, :]
    return np.concatenate([np.sin(angles), np.cos(angles)], axis=1).astype(np.float32)


def local(inners, outers, query_rot, key_rot, value_rows, attention_out, grad_out, log_norm,
          segments, block_table):
    del block_table
    tokens = query_rot.shape[1]
    rows = GROUP * tokens
    if segments.shape[0] > 1:
        example = lax.axis_index("outer") // KV_HEADS
        segments = lax.dynamic_slice_in_dim(segments, example, 1, 0)
    hbm = pl.BlockSpec(memory_space=pltpu.HBM)
    sems = pltpu.SemaphoreType.DMA
    shapes = (
        jax.ShapeDtypeStruct((tokens, GROUP * HEAD_DIM), BF16),
        jax.ShapeDtypeStruct((tokens, HEAD_DIM), BF16),
        jax.ShapeDtypeStruct((tokens, HEAD_DIM), BF16),
        jax.ShapeDtypeStruct((HEADS + 2 * KV_HEADS, HEAD_DIM), F32),
    )
    outs = pl.pallas_call(
        functools.partial(kernel, inners, outers),
        out_shape=shapes,
        in_specs=[hbm] * 9,
        out_specs=(hbm,) * 4,
        scratch_shapes=[
            pltpu.VMEM((tokens, HEAD_DIM), BF16),
            pltpu.VMEM((tokens, HEAD_DIM), BF16),
            pltpu.VMEM((1, tokens), jnp.int32),
            pltpu.VMEM((tokens, GROUP * HEAD_DIM), BF16),
            pltpu.VMEM((tokens, GROUP * HEAD_DIM), BF16),
            pltpu.VMEM((tokens, GROUP * HEAD_DIM), BF16),
            pltpu.VMEM((GROUP, 1, tokens), F32),
            pltpu.VMEM((tokens, HEAD_DIM), F32),
            pltpu.VMEM((inners, HEAD_DIM), F32),
            sems((9,)),
            pltpu.VMEM((tokens, GROUP * HEAD_DIM), BF16),
            pltpu.VMEM((tokens, HEAD_DIM), BF16),
            pltpu.VMEM((tokens, HEAD_DIM), BF16),
            pltpu.VMEM((HEADS + 2 * KV_HEADS, HEAD_DIM), F32),
            sems((4,)),
            pltpu.VMEM((inners, 3 * HEAD_DIM, tokens), BF16),
            pltpu.VMEM((rows, 2 * HEAD_DIM), BF16),
            pltpu.VMEM((rows, 2 * HEAD_DIM), BF16),
            pltpu.VMEM((HEAD_DIM, rows), BF16),
            pltpu.VMEM((HEAD_DIM, rows), BF16),
            pltpu.VMEM((rows, 2 * tokens), BF16),
            pltpu.VMEM((rows, 2 * tokens), BF16),
            pltpu.VMEM((rows, HEAD_DIM), F32),
            pltpu.VMEM((2 * HEAD_DIM, tokens), F32),
            pltpu.VMEM((inners // 2, 2 * HEAD_DIM, tokens), F32),
            pltpu.VMEM((inners // 2, 2 * HEAD_DIM, tokens), BF16),
            pltpu.VMEM((inners // 2, 2 * HEAD_DIM, tokens), BF16),
            pltpu.VMEM((inners, 2 * HEAD_DIM, tokens), BF16),
            pltpu.VMEM((inners, 2 * HEAD_DIM, tokens), BF16),
            pltpu.VMEM((HEAD_DIM, HEAD_DIM), F32),
            pltpu.VMEM((inners, HEAD_DIM), F32),
            pltpu.VMEM((BIAS_ROWS, HEAD_DIM), F32),
            pltpu.VMEM((inners, BIAS_ROWS, HEAD_DIM), F32),
            pltpu.VMEM((BIAS_ROWS, HEAD_DIM), F32),
            pltpu.VMEM((outers, BIAS_ROWS, HEAD_DIM), F32),
            sems((inners,)), sems((inners,)), sems((inners // 2,)), sems((inners // 2,)),
            sems((inners,)), sems((inners,)),
            sems((inners,)), sems((inners,)), sems((outers,)), sems((outers,)),
        ],
        compiler_params=pltpu.CompilerParams(
            collective_id=0, has_side_effects=True, vmem_limit_bytes=VMEM_LIMIT
        ),
        name="attention_backward",
    )(
        key_rot[0], value_rows[0], segments, query_rot[0], grad_out[0], attention_out[0],
        log_norm.reshape(GROUP, 1, tokens), jnp.asarray(rotary(np.arange(tokens))),
        jnp.asarray(rotary(np.arange(inners) * tokens)),
    )
    outs = pl.pallas_call(
        write,
        out_shape=shapes,
        in_specs=[hbm] * 4,
        out_specs=(hbm,) * 4,
        scratch_shapes=[pltpu.VMEM(shape.shape, shape.dtype) for shape in shapes] + [sems((8,))],
        compiler_params=pltpu.CompilerParams(vmem_limit_bytes=VMEM_LIMIT),
        name="write_results",
    )(*outs)
    return outs[0][None], outs[1][None], outs[2][None], outs[3].reshape(-1)


def solution(mesh):
    placed = (
        P("outer", "inner", None),
        P("outer", "inner", None),
        P("outer", "inner", None),
        P("outer", "inner", None),
        P("outer", "inner", None),
        P("outer", None, "inner"),
        P(None, "inner"),
        P(None, "inner", None),
    )
    return jax.shard_map(
        functools.partial(local, mesh.shape["inner"], mesh.shape["outer"]),
        mesh=mesh,
        in_specs=placed,
        out_specs=(
            P("outer", "inner", None),
            P("outer", "inner", None),
            P("outer", "inner", None),
            P(),
        ),
        check_vma=False,
    )
```

```python
import functools
import math

import jax
import jax.numpy as jnp
import numpy as np
from jax import lax
from jax.experimental import pallas as pl
from jax.experimental.pallas import tpu as pltpu
from jax.sharding import PartitionSpec as P

HEADS = 28
KV_HEADS = 4
HEAD_DIM = 128
GROUP = HEADS // KV_HEADS
ROPE_BASE = 1000000.0
ROOT = math.sqrt(HEAD_DIM)
SCALE = 1.0 / ROOT
MASKED = -1e30
EXTRA = 16
BIAS_ROWS = 16
VMEM_LIMIT = 63 * 1024 * 1024
MESH = pl.DeviceIdType.MESH
F32 = jnp.float32
BF16 = jnp.bfloat16


def partner(index, step, count):
    result = 0
    bit = 1
    while bit < count:
        result = result + ((index // bit + step // bit) % 2) * bit
        bit *= 2
    return result


def pieces(x):
    high = x.astype(BF16).astype(F32)
    rest = x - high
    middle = rest.astype(BF16).astype(F32)
    return high, middle, rest - middle


def dot(a, b):
    return jnp.dot(a, b, preferred_element_type=F32)


def kernel(
    inners, outers, k_hbm, v_hbm, seg_hbm, q_hbm, go_hbm, ao_hbm, norm_hbm, base_hbm, starts_hbm,
    dq_hbm, dk_hbm, dv_hbm, bias_hbm,
    k_ref, v_ref, seg_ref, q_ref, go_ref, ao_ref, norm_ref, base_ref, starts_ref, load_sem,
    dq_ref, dk_ref, dv_ref, bias_ref, store_sem,
    kv, q_aug, go_aug, q_t, go_t, probs, grads, dq_acc, own_acc, kept, pair_out, pair_in,
    part_out, part_in,
    sums, angles, bias_own, bias_in, plane_in,
    kv_send, kv_recv, pair_send, pair_recv, part_send, part_recv, bias_send, bias_recv, plane_send, plane_recv,
):
    tokens = k_ref.shape[0]
    rows = GROUP * tokens
    me = lax.axis_index("inner")
    plane = lax.axis_index("outer")

    loads = [
        pltpu.make_async_copy(source, target, load_sem.at[i])
        for i, (source, target) in enumerate([
            (k_hbm, k_ref), (v_hbm, v_ref), (seg_hbm, seg_ref), (q_hbm, q_ref), (go_hbm, go_ref),
            (ao_hbm, ao_ref), (norm_hbm, norm_ref), (base_hbm, base_ref), (starts_hbm, starts_ref),
        ])
    ]
    for load in loads:
        load.start()
    stores = [
        pltpu.make_async_copy(source, target, store_sem.at[i])
        for i, (source, target) in enumerate([
            (dq_ref, dq_hbm), (dk_ref, dk_hbm), (dv_ref, dv_hbm), (bias_ref, bias_hbm),
        ])
    ]

    def inner_id(step):
        return (plane, partner(me, step, inners))

    def beside(way):
        return (plane + way, me)

    has_left = plane > 0
    has_right = plane < outers - 1
    neighbours = (plane + outers - 1) // outers + (2 * outers - 2 - plane) // outers

    barrier = pltpu.get_barrier_semaphore()
    for step in range(1, inners):
        pl.semaphore_signal(barrier, inc=1, device_id=inner_id(step), device_id_type=MESH)

    @pl.when(has_left)
    def _():
        pl.semaphore_signal(barrier, inc=1, device_id=beside(-1), device_id_type=MESH)

    @pl.when(has_right)
    def _():
        pl.semaphore_signal(barrier, inc=1, device_id=beside(1), device_id_type=MESH)


    for load in loads[:3]:
        load.wait()
    seg = seg_ref[...].astype(F32)
    row = lax.broadcasted_iota(jnp.int32, (EXTRA, tokens), 0)
    seg_rows = jnp.broadcast_to(seg, (EXTRA, tokens))
    extra = jnp.where(row < 3, 1.0, 0.0)
    extra = jnp.where((row == 3) & (seg_rows == 1.0), 1.0, extra)
    extra = jnp.where((row == 4) & (seg_rows == 2.0), 1.0, extra)
    kv[0, :HEAD_DIM] = jnp.transpose(v_ref[...])
    kv[0, HEAD_DIM : 2 * HEAD_DIM] = jnp.transpose(k_ref[...])
    kv[0, 2 * HEAD_DIM : 2 * HEAD_DIM + EXTRA] = extra.astype(BF16)
    for slot in range(inners):
        kv[slot, 2 * HEAD_DIM + EXTRA :] = jnp.zeros((HEAD_DIM - EXTRA, tokens), BF16)

    pl.semaphore_wait(barrier, inners - 1 + neighbours)

    sent = 2 * HEAD_DIM + EXTRA

    def kv_copy(step):
        return pltpu.make_async_remote_copy(
            src_ref=kv.at[0, pl.ds(0, sent)],
            dst_ref=kv.at[step, pl.ds(0, sent)],
            send_sem=kv_send.at[step],
            recv_sem=kv_recv.at[step],
            device_id=inner_id(step),
            device_id_type=MESH,
        )

    def forward(step):
        return pltpu.make_async_remote_copy(
            src_ref=kv.at[step, pl.ds(0, sent)],
            dst_ref=kv.at[step + 1, pl.ds(0, sent)],
            send_sem=kv_send.at[step + 1],
            recv_sem=kv_recv.at[step + 1],
            device_id=inner_id(1),
            device_id_type=MESH,
        )

    def pair_copy(g):
        return pltpu.make_async_remote_copy(
            src_ref=pair_out.at[g],
            dst_ref=pair_in.at[g],
            send_sem=pair_send.at[g],
            recv_sem=pair_recv.at[g],
            device_id=inner_id(1),
            device_id_type=MESH,
        )

    def part_copy(step):
        return pltpu.make_async_remote_copy(
            src_ref=part_out.at[step],
            dst_ref=part_in.at[step],
            send_sem=part_send.at[step],
            recv_sem=part_recv.at[step],
            device_id=inner_id(step),
            device_id_type=MESH,
        )

    groups = inners // 2
    order = [1, 3, 2] if groups == 4 else list(range(1, groups))
    direct = [1] + [2 * g for g in range(1, groups)]
    for step in direct:
        kv_copy(step).start()

    for load in loads[3:]:
        load.wait()
    row8 = lax.broadcasted_iota(jnp.int32, (8, tokens), 0)
    seg8 = jnp.broadcast_to(seg, (8, tokens))
    masks = jnp.where((row8 == 3) & (seg8 != 1.0), MASKED, 0.0)
    masks = jnp.where((row8 == 4) & (seg8 != 2.0), MASKED, masks)
    lane = lax.broadcasted_iota(jnp.int32, (tokens, HEAD_DIM), 1)
    for g in range(GROUP):
        here = slice(g * tokens, (g + 1) * tokens)
        cols = slice(g * HEAD_DIM, (g + 1) * HEAD_DIM)
        query = q_ref[:, cols]
        grad = go_ref[:, cols]
        q_aug[here, :HEAD_DIM] = query
        go_aug[here, :HEAD_DIM] = grad
        q_t[:, here] = jnp.transpose(query)
        go_t[:, here] = jnp.transpose(grad)
        high, middle, low = pieces(norm_ref[g] * -ROOT)
        top = jnp.where(row8 == 0, high, masks)
        top = jnp.where(row8 == 1, middle, top)
        top = jnp.where(row8 == 2, low, top)
        full = jnp.concatenate([top, jnp.zeros((HEAD_DIM - 8, tokens), F32)], axis=0)
        q_aug[here, HEAD_DIM:] = jnp.transpose(full).astype(BF16)
        delta = -jnp.sum(
            grad.astype(F32) * ao_ref[:, cols].astype(F32), axis=1, keepdims=True
        )
        d_high, d_middle, d_low = pieces(delta)
        side = jnp.where(lane == 0, d_high, 0.0)
        side = jnp.where(lane == 1, d_middle, side)
        side = jnp.where(lane == 2, d_low, side)
        go_aug[here, HEAD_DIM:] = side.astype(BF16)

    half = HEAD_DIM // 2
    for slot in range(inners):
        angles[slot : slot + 1] = starts_ref[pl.ds(partner(me, slot, inners), 1)]

    def both(table):
        below = lax.broadcasted_iota(jnp.int32, table.shape, 1) < half
        turned = pltpu.roll(table, half, 1)
        return jnp.where(below, turned, table), jnp.where(below, table, -turned)

    base_cos, base_sin = both(base_ref[...])
    start_cos, start_sin = both(angles[...])
    cosine = base_cos * start_cos[:1] - base_sin * start_sin[:1]
    sine = base_sin * start_cos[:1] + base_cos * start_sin[:1]
    base_t = jnp.transpose(base_ref[...])
    sine_t, cosine_t = base_t[:half], base_t[half:]
    sums[...] = jnp.zeros((HEAD_DIM, HEAD_DIM), F32)
    sum_lane = lax.broadcasted_iota(jnp.int32, (HEAD_DIM, HEAD_DIM), 1)

    def unrotate(x):
        return x * cosine + pltpu.roll(x, half, 1) * sine

    chunk = rows if tokens <= 128 else 256
    starts = list(range(0, rows, chunk))

    def compute(g, first):
        block = jnp.concatenate([kv[2 * g], kv[2 * g + 1]], axis=1)
        values_t = jnp.concatenate([block[:HEAD_DIM], block[2 * HEAD_DIM :]], axis=0)
        keys_t = block[HEAD_DIM:]
        keys = jnp.transpose(block[HEAD_DIM : 2 * HEAD_DIM])
        for start in starts:
            here = slice(start, min(start + chunk, rows))
            scores = dot(q_aug[here], keys_t)
            chances = jnp.exp(scores * SCALE)
            probs[here] = chances.astype(BF16)
            low_grads = (chances * dot(go_aug[here], values_t)).astype(BF16)
            grads[here] = low_grads
            part = dot(low_grads, keys)
            if first:
                dq_acc[here] = part
            else:
                dq_acc[here] += part
        value_part = dot(go_t[...], probs[...])
        key_part = dot(q_t[...], grads[...])
        return key_part, value_part

    def count(slot, key_part, value_part):
        upper, lower = key_part[:half], key_part[half:]
        key_sum = jnp.concatenate(
            [
                jnp.sum(upper * cosine_t + lower * sine_t, axis=1, keepdims=True),
                jnp.sum(lower * cosine_t - upper * sine_t, axis=1, keepdims=True),
            ],
            axis=0,
        )
        value_sum = jnp.sum(value_part, axis=1, keepdims=True)
        held = jnp.where(sum_lane == slot, key_sum, sums[...])
        sums[...] = jnp.where(sum_lane == half + slot, value_sum, held)

    def pass_on(g):
        kv_copy(2 * g).wait_recv()
        forward(2 * g).start()

    def turn(g):
        forward(2 * g).wait_recv()
        key_part, value_part = compute(g, False)
        pair_out[g, :HEAD_DIM] = key_part[:, tokens:].astype(BF16)
        pair_out[g, HEAD_DIM:] = value_part[:, tokens:].astype(BF16)
        pair_copy(g).start()
        kept[g, :HEAD_DIM] = key_part[:, :tokens]
        kept[g, HEAD_DIM:] = value_part[:, :tokens]
        count(2 * g, key_part[:, :tokens], value_part[:, :tokens])
        count(2 * g + 1, key_part[:, tokens:], value_part[:, tokens:])

    def send_home(g):
        pair_copy(g).wait_recv()
        part_out[2 * g] = (kept[g] + pair_in[g].astype(F32)).astype(BF16)
        part_copy(2 * g).start()

    kv_copy(1).wait_recv()
    key_part, value_part = compute(0, True)
    part_out[1, :HEAD_DIM] = key_part[:, tokens:].astype(BF16)
    part_out[1, HEAD_DIM:] = value_part[:, tokens:].astype(BF16)
    part_copy(1).start()
    own_acc[:HEAD_DIM] = key_part[:, :tokens]
    own_acc[HEAD_DIM:] = value_part[:, :tokens]
    count(0, key_part[:, :tokens], value_part[:, :tokens])
    count(1, key_part[:, tokens:], value_part[:, tokens:])
    if groups <= 4:
        for i, g in enumerate(order):
            if i == 0:
                pass_on(g)
            if i + 1 < len(order):
                pass_on(order[i + 1])
            turn(g)
            if i > 0:
                send_home(order[i - 1])
    else:

        def whole_turn(g, carry):
            pass_on(g)
            turn(g)
            send_home(g)
            return carry

        lax.fori_loop(1, groups, whole_turn, 0)

    bias_own[...] = jnp.zeros((BIAS_ROWS, HEAD_DIM), F32)
    for g in range(GROUP):
        full = unrotate(dq_acc[g * tokens : (g + 1) * tokens] * SCALE)
        dq_ref[:, g * HEAD_DIM : (g + 1) * HEAD_DIM] = full.astype(BF16)
        bias_own[g : g + 1] = jnp.sum(full, axis=0, keepdims=True)
    stores[0].start()

    sums_t = jnp.transpose(sums[...])
    key_sums = sums_t[:inners]
    key_sums = key_sums * start_cos + pltpu.roll(key_sums, half, 1) * start_sin
    bias_own[GROUP : GROUP + 1] = jnp.sum(key_sums, axis=0, keepdims=True) * SCALE
    bias_own[GROUP + 1 : GROUP + 2] = jnp.sum(sums_t[half : half + inners], axis=0, keepdims=True)

    def bias_copy(step, slot):
        return pltpu.make_async_remote_copy(
            src_ref=bias_own,
            dst_ref=bias_in.at[slot],
            send_sem=bias_send.at[step],
            recv_sem=bias_recv.at[step],
            device_id=inner_id(step),
            device_id_type=MESH,
        )

    def rightward(far, slot):
        return pltpu.make_async_remote_copy(
            src_ref=plane_in.at[slot],
            dst_ref=plane_in.at[slot],
            send_sem=plane_send.at[far],
            recv_sem=plane_recv.at[far],
            device_id=beside(1),
            device_id_type=MESH,
        )

    def leftward(far, slot):
        return pltpu.make_async_remote_copy(
            src_ref=plane_in.at[slot],
            dst_ref=plane_in.at[slot],
            send_sem=plane_send.at[outers + far],
            recv_sem=plane_recv.at[outers + far],
            device_id=beside(-1),
            device_id_type=MESH,
        )

    def send_right(far, act):
        @pl.when((plane - far + 1 >= 0) & has_right)
        def _():
            act(rightward(far, plane - far + 1))

    def send_left(far, act):
        @pl.when((plane + far - 1 < outers) & has_left)
        def _():
            act(leftward(far, plane + far - 1))

    for step in range(1, inners):
        bias_copy(step, me).start()
    if groups <= 4:
        send_home(order[-1])
    bias_in[me] = bias_own[...]
    for step in range(1, inners):
        bias_copy(step, partner(me, step, inners)).wait_recv()
    summed = bias_in[0]
    for slot in range(1, inners):
        summed = summed + bias_in[slot]
    plane_in[plane] = summed
    send_right(1, lambda copy: copy.start())
    send_left(1, lambda copy: copy.start())

    total = own_acc[...]
    for step in direct:
        part_copy(step).wait_recv()
        total = total + part_in[step].astype(F32)
    key_full = unrotate(jnp.transpose(total[:HEAD_DIM]) * SCALE)
    value_full = jnp.transpose(total[HEAD_DIM:])
    dk_ref[...] = key_full.astype(BF16)
    dv_ref[...] = value_full.astype(BF16)
    stores[1].start()
    stores[2].start()

    for far in range(1, outers):

        @pl.when(plane - far >= 0)
        def _(far=far):
            rightward(far, plane - far).wait_recv()

        if far + 1 < outers:
            send_right(far + 1, lambda copy: copy.start())

        @pl.when(plane + far < outers)
        def _(far=far):
            leftward(far, plane + far).wait_recv()

        if far + 1 < outers:
            send_left(far + 1, lambda copy: copy.start())
    for head in range(KV_HEADS):
        whole = plane_in[head]
        for other in range(head + KV_HEADS, outers, KV_HEADS):
            whole = whole + plane_in[other]
        bias_ref[head * GROUP : (head + 1) * GROUP] = whole[:GROUP]
        bias_ref[HEADS + head : HEADS + head + 1] = whole[GROUP : GROUP + 1]
        at = HEADS + KV_HEADS + head
        bias_ref[at : at + 1] = whole[GROUP + 1 : GROUP + 2]
    stores[3].start()

    for step in direct:
        kv_copy(step).wait_send()
        part_copy(step).wait_send()
    for g in range(1, groups):
        forward(2 * g).wait_send()
        pair_copy(g).wait_send()
    for step in range(1, inners):
        bias_copy(step, me).wait_send()
    for far in range(1, outers):
        send_right(far, lambda copy: copy.wait_send())
        send_left(far, lambda copy: copy.wait_send())
    for store in stores:
        store.wait()


def write(*refs):
    sources, targets, held, sem = refs[:4], refs[4:8], refs[8:12], refs[12]
    loads = [pltpu.make_async_copy(sources[i], held[i], sem.at[i]) for i in range(4)]
    stores = [pltpu.make_async_copy(held[i], targets[i], sem.at[4 + i]) for i in range(4)]
    for load in loads:
        load.start()
    for load, store in zip(loads, stores):
        load.wait()
        store.start()
    for store in stores:
        store.wait()


def rotary(positions):
    frequency = np.exp(np.arange(HEAD_DIM // 2) * (-2.0 * math.log(ROPE_BASE) / HEAD_DIM))
    angles = np.asarray(positions)[:, None] * frequency[None, :]
    return np.concatenate([np.sin(angles), np.cos(angles)], axis=1).astype(np.float32)


def local(inners, outers, query_rot, key_rot, value_rows, attention_out, grad_out, log_norm,
          segments, block_table):
    del block_table
    tokens = query_rot.shape[1]
    rows = GROUP * tokens
    if segments.shape[0] > 1:
        example = lax.axis_index("outer") // KV_HEADS
        segments = lax.dynamic_slice_in_dim(segments, example, 1, 0)
    hbm = pl.BlockSpec(memory_space=pltpu.HBM)
    sems = pltpu.SemaphoreType.DMA
    shapes = (
        jax.ShapeDtypeStruct((tokens, GROUP * HEAD_DIM), BF16),
        jax.ShapeDtypeStruct((tokens, HEAD_DIM), BF16),
        jax.ShapeDtypeStruct((tokens, HEAD_DIM), BF16),
        jax.ShapeDtypeStruct((HEADS + 2 * KV_HEADS, HEAD_DIM), F32),
    )
    outs = pl.pallas_call(
        functools.partial(kernel, inners, outers),
        out_shape=shapes,
        in_specs=[hbm] * 9,
        out_specs=(hbm,) * 4,
        scratch_shapes=[
            pltpu.VMEM((tokens, HEAD_DIM), BF16),
            pltpu.VMEM((tokens, HEAD_DIM), BF16),
            pltpu.VMEM((1, tokens), jnp.int32),
            pltpu.VMEM((tokens, GROUP * HEAD_DIM), BF16),
            pltpu.VMEM((tokens, GROUP * HEAD_DIM), BF16),
            pltpu.VMEM((tokens, GROUP * HEAD_DIM), BF16),
            pltpu.VMEM((GROUP, 1, tokens), F32),
            pltpu.VMEM((tokens, HEAD_DIM), F32),
            pltpu.VMEM((inners, HEAD_DIM), F32),
            sems((9,)),
            pltpu.VMEM((tokens, GROUP * HEAD_DIM), BF16),
            pltpu.VMEM((tokens, HEAD_DIM), BF16),
            pltpu.VMEM((tokens, HEAD_DIM), BF16),
            pltpu.VMEM((HEADS + 2 * KV_HEADS, HEAD_DIM), F32),
            sems((4,)),
            pltpu.VMEM((inners, 3 * HEAD_DIM, tokens), BF16),
            pltpu.VMEM((rows, 2 * HEAD_DIM), BF16),
            pltpu.VMEM((rows, 2 * HEAD_DIM), BF16),
            pltpu.VMEM((HEAD_DIM, rows), BF16),
            pltpu.VMEM((HEAD_DIM, rows), BF16),
            pltpu.VMEM((rows, 2 * tokens), BF16),
            pltpu.VMEM((rows, 2 * tokens), BF16),
            pltpu.VMEM((rows, HEAD_DIM), F32),
            pltpu.VMEM((2 * HEAD_DIM, tokens), F32),
            pltpu.VMEM((inners // 2, 2 * HEAD_DIM, tokens), F32),
            pltpu.VMEM((inners // 2, 2 * HEAD_DIM, tokens), BF16),
            pltpu.VMEM((inners // 2, 2 * HEAD_DIM, tokens), BF16),
            pltpu.VMEM((inners, 2 * HEAD_DIM, tokens), BF16),
            pltpu.VMEM((inners, 2 * HEAD_DIM, tokens), BF16),
            pltpu.VMEM((HEAD_DIM, HEAD_DIM), F32),
            pltpu.VMEM((inners, HEAD_DIM), F32),
            pltpu.VMEM((BIAS_ROWS, HEAD_DIM), F32),
            pltpu.VMEM((inners, BIAS_ROWS, HEAD_DIM), F32),
            pltpu.VMEM((outers, BIAS_ROWS, HEAD_DIM), F32),
            sems((inners,)), sems((inners,)), sems((inners // 2,)), sems((inners // 2,)),
            sems((inners,)), sems((inners,)),
            sems((inners,)), sems((inners,)), sems((2 * outers,)), sems((2 * outers,)),
        ],
        compiler_params=pltpu.CompilerParams(
            collective_id=0, has_side_effects=True, vmem_limit_bytes=VMEM_LIMIT
        ),
        name="attention_backward",
    )(
        key_rot[0], value_rows[0], segments, query_rot[0], grad_out[0], attention_out[0],
        log_norm.reshape(GROUP, 1, tokens), jnp.asarray(rotary(np.arange(tokens))),
        jnp.asarray(rotary(np.arange(inners) * tokens)),
    )
    outs = pl.pallas_call(
        write,
        out_shape=shapes,
        in_specs=[hbm] * 4,
        out_specs=(hbm,) * 4,
        scratch_shapes=[pltpu.VMEM(shape.shape, shape.dtype) for shape in shapes] + [sems((8,))],
        compiler_params=pltpu.CompilerParams(vmem_limit_bytes=VMEM_LIMIT),
        name="write_results",
    )(*outs)
    return outs[0][None], outs[1][None], outs[2][None], outs[3].reshape(-1)


def solution(mesh):
    placed = (
        P("outer", "inner", None),
        P("outer", "inner", None),
        P("outer", "inner", None),
        P("outer", "inner", None),
        P("outer", "inner", None),
        P("outer", None, "inner"),
        P(None, "inner"),
        P(None, "inner", None),
    )
    return jax.shard_map(
        functools.partial(local, mesh.shape["inner"], mesh.shape["outer"]),
        mesh=mesh,
        in_specs=placed,
        out_specs=(
            P("outer", "inner", None),
            P("outer", "inner", None),
            P("outer", "inner", None),
            P(),
        ),
        check_vma=False,
    )
```

```python
import functools
import math

import jax
import jax.numpy as jnp
import numpy as np
from jax import lax
from jax.experimental import pallas as pl
from jax.experimental.pallas import tpu as pltpu
from jax.sharding import PartitionSpec as P

HEADS = 28
KV_HEADS = 4
HEAD_DIM = 128
GROUP = HEADS // KV_HEADS
ROPE_BASE = 1000000.0
ROOT = math.sqrt(HEAD_DIM)
SCALE = 1.0 / ROOT
MASKED = -1e30
EXTRA = 16
BIAS_ROWS = 16
VMEM_LIMIT = 63 * 1024 * 1024
MESH = pl.DeviceIdType.MESH
F32 = jnp.float32
BF16 = jnp.bfloat16


def partner(index, step, count):
    result = 0
    bit = 1
    while bit < count:
        result = result + ((index // bit + step // bit) % 2) * bit
        bit *= 2
    return result


def pieces(x):
    high = x.astype(BF16).astype(F32)
    rest = x - high
    middle = rest.astype(BF16).astype(F32)
    return high, middle, rest - middle


def dot(a, b):
    return jnp.dot(a, b, preferred_element_type=F32)


def kernel(
    inners, outers, k_hbm, v_hbm, seg_hbm, q_hbm, go_hbm, ao_hbm, norm_hbm, base_hbm, starts_hbm,
    dq_hbm, dk_hbm, dv_hbm, bias_hbm,
    k_ref, v_ref, seg_ref, q_ref, go_ref, ao_ref, norm_ref, base_ref, starts_ref, load_sem,
    dq_ref, dk_ref, dv_ref, bias_ref, store_sem,
    kv, q_aug, go_aug, q_t, go_t, probs, grads, dq_acc, own_acc, kept, pair_out, pair_in,
    part_out, part_in,
    prob_sums, angles, bias_own, bias_in, plane_own, plane_in,
    kv_send, kv_recv, pair_send, pair_recv, part_send, part_recv, bias_send, bias_recv, plane_send, plane_recv,
):
    tokens = k_ref.shape[0]
    rows = GROUP * tokens
    me = lax.axis_index("inner")
    plane = lax.axis_index("outer")

    loads = [
        pltpu.make_async_copy(source, target, load_sem.at[i])
        for i, (source, target) in enumerate([
            (k_hbm, k_ref), (v_hbm, v_ref), (seg_hbm, seg_ref), (q_hbm, q_ref), (go_hbm, go_ref),
            (ao_hbm, ao_ref), (norm_hbm, norm_ref), (base_hbm, base_ref), (starts_hbm, starts_ref),
        ])
    ]
    for load in loads:
        load.start()
    stores = [
        pltpu.make_async_copy(source, target, store_sem.at[i])
        for i, (source, target) in enumerate([
            (dq_ref, dq_hbm), (dk_ref, dk_hbm), (dv_ref, dv_hbm), (bias_ref, bias_hbm),
        ])
    ]

    def inner_id(step):
        return (plane, partner(me, step, inners))

    def outer_id(step):
        return (partner(plane, step, outers), me)

    barrier = pltpu.get_barrier_semaphore()
    for step in range(1, inners):
        pl.semaphore_signal(barrier, inc=1, device_id=inner_id(step), device_id_type=MESH)
    for step in range(1, outers):
        pl.semaphore_signal(barrier, inc=1, device_id=outer_id(step), device_id_type=MESH)

    for load in loads[:3]:
        load.wait()
    seg = seg_ref[...].astype(F32)
    row = lax.broadcasted_iota(jnp.int32, (EXTRA, tokens), 0)
    seg_rows = jnp.broadcast_to(seg, (EXTRA, tokens))
    extra = jnp.where(row < 3, 1.0, 0.0)
    extra = jnp.where((row == 3) & (seg_rows == 1.0), 1.0, extra)
    extra = jnp.where((row == 4) & (seg_rows == 2.0), 1.0, extra)
    kv[0, :HEAD_DIM] = jnp.transpose(v_ref[...])
    kv[0, HEAD_DIM : 2 * HEAD_DIM] = jnp.transpose(k_ref[...])
    kv[0, 2 * HEAD_DIM : 2 * HEAD_DIM + EXTRA] = extra.astype(BF16)
    for slot in range(inners):
        kv[slot, 2 * HEAD_DIM + EXTRA :] = jnp.zeros((HEAD_DIM - EXTRA, tokens), BF16)

    pl.semaphore_wait(barrier, inners + outers - 2)

    sent = 2 * HEAD_DIM + EXTRA

    def kv_copy(step):
        return pltpu.make_async_remote_copy(
            src_ref=kv.at[0, pl.ds(0, sent)],
            dst_ref=kv.at[step, pl.ds(0, sent)],
            send_sem=kv_send.at[step],
            recv_sem=kv_recv.at[step],
            device_id=inner_id(step),
            device_id_type=MESH,
        )

    def forward(step):
        return pltpu.make_async_remote_copy(
            src_ref=kv.at[step, pl.ds(0, sent)],
            dst_ref=kv.at[step + 1, pl.ds(0, sent)],
            send_sem=kv_send.at[step + 1],
            recv_sem=kv_recv.at[step + 1],
            device_id=inner_id(1),
            device_id_type=MESH,
        )

    def pair_copy(g):
        return pltpu.make_async_remote_copy(
            src_ref=pair_out.at[g],
            dst_ref=pair_in.at[g],
            send_sem=pair_send.at[g],
            recv_sem=pair_recv.at[g],
            device_id=inner_id(1),
            device_id_type=MESH,
        )

    def part_copy(step):
        return pltpu.make_async_remote_copy(
            src_ref=part_out.at[step],
            dst_ref=part_in.at[step],
            send_sem=part_send.at[step],
            recv_sem=part_recv.at[step],
            device_id=inner_id(step),
            device_id_type=MESH,
        )

    groups = inners // 2
    direct = [1] + [2 * g for g in range(1, groups)]
    for step in direct:
        kv_copy(step).start()

    for load in loads[3:]:
        load.wait()
    row8 = lax.broadcasted_iota(jnp.int32, (8, tokens), 0)
    seg8 = jnp.broadcast_to(seg, (8, tokens))
    masks = jnp.where((row8 == 3) & (seg8 != 1.0), MASKED, 0.0)
    masks = jnp.where((row8 == 4) & (seg8 != 2.0), MASKED, masks)
    lane = lax.broadcasted_iota(jnp.int32, (tokens, HEAD_DIM), 1)
    for g in range(GROUP):
        here = slice(g * tokens, (g + 1) * tokens)
        cols = slice(g * HEAD_DIM, (g + 1) * HEAD_DIM)
        query = q_ref[:, cols]
        grad = go_ref[:, cols]
        q_aug[here, :HEAD_DIM] = query
        go_aug[here, :HEAD_DIM] = grad
        q_t[:, here] = jnp.transpose(query)
        go_t[:, here] = jnp.transpose(grad)
        high, middle, low = pieces(norm_ref[g] * -ROOT)
        top = jnp.where(row8 == 0, high, masks)
        top = jnp.where(row8 == 1, middle, top)
        top = jnp.where(row8 == 2, low, top)
        full = jnp.concatenate([top, jnp.zeros((HEAD_DIM - 8, tokens), F32)], axis=0)
        q_aug[here, HEAD_DIM:] = jnp.transpose(full).astype(BF16)
        delta = -jnp.sum(
            grad.astype(F32) * ao_ref[:, cols].astype(F32), axis=1, keepdims=True
        )
        d_high, d_middle, d_low = pieces(delta)
        side = jnp.where(lane == 0, d_high, 0.0)
        side = jnp.where(lane == 1, d_middle, side)
        side = jnp.where(lane == 2, d_low, side)
        go_aug[here, HEAD_DIM:] = side.astype(BF16)

    half = HEAD_DIM // 2
    for slot in range(inners):
        angles[slot : slot + 1] = starts_ref[pl.ds(partner(me, slot, inners), 1)]

    def both(table):
        below = lax.broadcasted_iota(jnp.int32, table.shape, 1) < half
        turned = pltpu.roll(table, half, 1)
        return jnp.where(below, turned, table), jnp.where(below, table, -turned)

    base_cos, base_sin = both(base_ref[...])
    start_cos, start_sin = both(angles[...])
    cosine = base_cos * start_cos[:1] - base_sin * start_sin[:1]
    sine = base_sin * start_cos[:1] + base_cos * start_sin[:1]
    base_turned = pltpu.roll(base_ref[...], half, 1)

    def waves(slot):
        start_cos, start_sin = both(angles[pl.ds(slot, 1)])
        return (base_ref[...] * start_cos + base_turned * start_sin).astype(BF16)

    def unrotate(x):
        return x * cosine + pltpu.roll(x, half, 1) * sine

    chunk = rows if tokens <= 128 else 256
    starts = list(range(0, rows, chunk))

    def query_side(g, first):
        block = jnp.concatenate([kv[2 * g], kv[2 * g + 1]], axis=1)
        values_t = jnp.concatenate([block[:HEAD_DIM], block[2 * HEAD_DIM :]], axis=0)
        keys_t = block[HEAD_DIM:]
        turns = jnp.concatenate([waves(2 * g), waves(2 * g + 1)], axis=0)
        keys = jnp.concatenate([jnp.transpose(block[HEAD_DIM : 2 * HEAD_DIM]), turns], axis=1)
        for start in starts:
            here = slice(start, min(start + chunk, rows))
            chances = jnp.exp(dot(q_aug[here], keys_t) * SCALE)
            probs[g, here] = chances.astype(BF16)
            low_grads = (chances * dot(go_aug[here], values_t)).astype(BF16)
            grads[g, here] = low_grads
            part = dot(low_grads, keys)
            chance_part = chances[:, :HEAD_DIM]
            for col in range(HEAD_DIM, 2 * tokens, HEAD_DIM):
                chance_part = chance_part + chances[:, col : col + HEAD_DIM]
            if first:
                dq_acc[here] = part
                prob_sums[here] = chance_part
            else:
                dq_acc[here] += part
                prob_sums[here] += chance_part

    def key_side(g):
        return dot(q_t[...], grads[g]), dot(go_t[...], probs[g])

    def pass_on(g):
        kv_copy(2 * g).wait_recv()
        forward(2 * g).start()

    def turn(g):
        forward(2 * g).wait_recv()
        query_side(g, False)

    def give(g):
        key_part, value_part = key_side(g)
        pair_out[g, :HEAD_DIM] = key_part[:, tokens:].astype(BF16)
        pair_out[g, HEAD_DIM:] = value_part[:, tokens:].astype(BF16)
        pair_copy(g).start()
        kept[g, :HEAD_DIM] = key_part[:, :tokens]
        kept[g, HEAD_DIM:] = value_part[:, :tokens]

    def send_home(g):
        pair_copy(g).wait_recv()
        part_out[2 * g] = (kept[g] + pair_in[g].astype(F32)).astype(BF16)
        part_copy(2 * g).start()

    kv_copy(1).wait_recv()
    query_side(0, True)
    if groups == 4:
        pass_on(1)
        pass_on(3)
        turn(1)
        pass_on(2)
        turn(3)
        give(1)
        turn(2)
        send_home(1)
    else:

        def whole_turn(g, carry):
            pass_on(g)
            turn(g)
            return carry

        lax.fori_loop(1, groups, whole_turn, 0)

    bias_own[...] = jnp.zeros((BIAS_ROWS, HEAD_DIM), F32)
    key_bias = jnp.zeros((tokens, HEAD_DIM), F32)
    value_bias = jnp.zeros((tokens, HEAD_DIM), F32)
    for g in range(GROUP):
        here = slice(g * tokens, (g + 1) * tokens)
        cols = slice(g * HEAD_DIM, (g + 1) * HEAD_DIM)
        full = unrotate(dq_acc[here, :HEAD_DIM] * SCALE)
        dq_ref[:, cols] = full.astype(BF16)
        bias_own[g : g + 1] = jnp.sum(full, axis=0, keepdims=True)
        query = q_ref[:, cols].astype(F32)
        turn_cos, turn_sin = both(dq_acc[here, HEAD_DIM:])
        key_bias = key_bias + query * turn_cos + pltpu.roll(query, half, 1) * turn_sin
        weight = jnp.sum(prob_sums[here], axis=1, keepdims=True)
        value_bias = value_bias + weight * go_ref[:, cols].astype(F32)
    bias_own[GROUP : GROUP + 1] = jnp.sum(key_bias, axis=0, keepdims=True) * SCALE
    bias_own[GROUP + 1 : GROUP + 2] = jnp.sum(value_bias, axis=0, keepdims=True)

    def bias_copy(step, slot):
        return pltpu.make_async_remote_copy(
            src_ref=bias_own,
            dst_ref=bias_in.at[slot],
            send_sem=bias_send.at[step],
            recv_sem=bias_recv.at[step],
            device_id=inner_id(step),
            device_id_type=MESH,
        )

    def plane_copy(step, slot):
        return pltpu.make_async_remote_copy(
            src_ref=plane_own,
            dst_ref=plane_in.at[slot],
            send_sem=plane_send.at[step],
            recv_sem=plane_recv.at[step],
            device_id=outer_id(step),
            device_id_type=MESH,
        )

    def bias_along():
        for step in range(1, inners):
            bias_copy(step, partner(me, step, inners)).wait_recv()
        summed = bias_in[0]
        for slot in range(1, inners):
            summed = summed + bias_in[slot]
        plane_own[...] = summed
        for step in range(1, outers):
            plane_copy(step, plane).start()
        plane_in[plane] = summed

    for step in range(1, inners):
        bias_copy(step, me).start()
    stores[0].start()
    bias_in[me] = bias_own[...]
    if groups == 4:
        give(3)
        give(2)
        send_home(3)
        bias_along()
    else:

        def whole_give(g, carry):
            give(g)
            send_home(g)
            return carry

        lax.fori_loop(1, groups, whole_give, 0)
        bias_along()
    key_part, value_part = key_side(0)
    part_out[1, :HEAD_DIM] = key_part[:, tokens:].astype(BF16)
    part_out[1, HEAD_DIM:] = value_part[:, tokens:].astype(BF16)
    part_copy(1).start()
    if groups == 4:
        send_home(2)
    own_acc[:HEAD_DIM] = key_part[:, :tokens]
    own_acc[HEAD_DIM:] = value_part[:, :tokens]

    total = own_acc[...]
    for step in direct:
        part_copy(step).wait_recv()
        total = total + part_in[step].astype(F32)
    key_full = unrotate(jnp.transpose(total[:HEAD_DIM]) * SCALE)
    value_full = jnp.transpose(total[HEAD_DIM:])
    dk_ref[...] = key_full.astype(BF16)
    dv_ref[...] = value_full.astype(BF16)
    stores[1].start()
    stores[2].start()

    for step in range(1, outers):
        plane_copy(step, partner(plane, step, outers)).wait_recv()
    for head in range(KV_HEADS):
        whole = plane_in[head]
        for other in range(head + KV_HEADS, outers, KV_HEADS):
            whole = whole + plane_in[other]
        bias_ref[head * GROUP : (head + 1) * GROUP] = whole[:GROUP]
        bias_ref[HEADS + head : HEADS + head + 1] = whole[GROUP : GROUP + 1]
        at = HEADS + KV_HEADS + head
        bias_ref[at : at + 1] = whole[GROUP + 1 : GROUP + 2]
    stores[3].start()

    for step in direct:
        kv_copy(step).wait_send()
        part_copy(step).wait_send()
    for g in range(1, groups):
        forward(2 * g).wait_send()
        pair_copy(g).wait_send()
    for step in range(1, inners):
        bias_copy(step, me).wait_send()
    for step in range(1, outers):
        plane_copy(step, plane).wait_send()
    for store in stores:
        store.wait()


def write(*refs):
    sources, targets, held, sem = refs[:4], refs[4:8], refs[8:12], refs[12]
    loads = [pltpu.make_async_copy(sources[i], held[i], sem.at[i]) for i in range(4)]
    stores = [pltpu.make_async_copy(held[i], targets[i], sem.at[4 + i]) for i in range(4)]
    for load in loads:
        load.start()
    for load, store in zip(loads, stores):
        load.wait()
        store.start()
    for store in stores:
        store.wait()


def rotary(positions):
    frequency = np.exp(np.arange(HEAD_DIM // 2) * (-2.0 * math.log(ROPE_BASE) / HEAD_DIM))
    angles = np.asarray(positions)[:, None] * frequency[None, :]
    return np.concatenate([np.sin(angles), np.cos(angles)], axis=1).astype(np.float32)


def local(inners, outers, query_rot, key_rot, value_rows, attention_out, grad_out, log_norm,
          segments, block_table):
    del block_table
    tokens = query_rot.shape[1]
    rows = GROUP * tokens
    if segments.shape[0] > 1:
        example = lax.axis_index("outer") // KV_HEADS
        segments = lax.dynamic_slice_in_dim(segments, example, 1, 0)
    hbm = pl.BlockSpec(memory_space=pltpu.HBM)
    sems = pltpu.SemaphoreType.DMA
    shapes = (
        jax.ShapeDtypeStruct((tokens, GROUP * HEAD_DIM), BF16),
        jax.ShapeDtypeStruct((tokens, HEAD_DIM), BF16),
        jax.ShapeDtypeStruct((tokens, HEAD_DIM), BF16),
        jax.ShapeDtypeStruct((HEADS + 2 * KV_HEADS, HEAD_DIM), F32),
    )
    outs = pl.pallas_call(
        functools.partial(kernel, inners, outers),
        out_shape=shapes,
        in_specs=[hbm] * 9,
        out_specs=(hbm,) * 4,
        scratch_shapes=[
            pltpu.VMEM((tokens, HEAD_DIM), BF16),
            pltpu.VMEM((tokens, HEAD_DIM), BF16),
            pltpu.VMEM((1, tokens), jnp.int32),
            pltpu.VMEM((tokens, GROUP * HEAD_DIM), BF16),
            pltpu.VMEM((tokens, GROUP * HEAD_DIM), BF16),
            pltpu.VMEM((tokens, GROUP * HEAD_DIM), BF16),
            pltpu.VMEM((GROUP, 1, tokens), F32),
            pltpu.VMEM((tokens, HEAD_DIM), F32),
            pltpu.VMEM((inners, HEAD_DIM), F32),
            sems((9,)),
            pltpu.VMEM((tokens, GROUP * HEAD_DIM), BF16),
            pltpu.VMEM((tokens, HEAD_DIM), BF16),
            pltpu.VMEM((tokens, HEAD_DIM), BF16),
            pltpu.VMEM((HEADS + 2 * KV_HEADS, HEAD_DIM), F32),
            sems((4,)),
            pltpu.VMEM((inners, 3 * HEAD_DIM, tokens), BF16),
            pltpu.VMEM((rows, 2 * HEAD_DIM), BF16),
            pltpu.VMEM((rows, 2 * HEAD_DIM), BF16),
            pltpu.VMEM((HEAD_DIM, rows), BF16),
            pltpu.VMEM((HEAD_DIM, rows), BF16),
            pltpu.VMEM((inners // 2, rows, 2 * tokens), BF16),
            pltpu.VMEM((inners // 2, rows, 2 * tokens), BF16),
            pltpu.VMEM((rows, 2 * HEAD_DIM), F32),
            pltpu.VMEM((2 * HEAD_DIM, tokens), F32),
            pltpu.VMEM((inners // 2, 2 * HEAD_DIM, tokens), F32),
            pltpu.VMEM((inners // 2, 2 * HEAD_DIM, tokens), BF16),
            pltpu.VMEM((inners // 2, 2 * HEAD_DIM, tokens), BF16),
            pltpu.VMEM((inners, 2 * HEAD_DIM, tokens), BF16),
            pltpu.VMEM((inners, 2 * HEAD_DIM, tokens), BF16),
            pltpu.VMEM((rows, HEAD_DIM), F32),
            pltpu.VMEM((inners, HEAD_DIM), F32),
            pltpu.VMEM((BIAS_ROWS, HEAD_DIM), F32),
            pltpu.VMEM((inners, BIAS_ROWS, HEAD_DIM), F32),
            pltpu.VMEM((BIAS_ROWS, HEAD_DIM), F32),
            pltpu.VMEM((outers, BIAS_ROWS, HEAD_DIM), F32),
            sems((inners,)), sems((inners,)), sems((inners // 2,)), sems((inners // 2,)),
            sems((inners,)), sems((inners,)),
            sems((inners,)), sems((inners,)), sems((outers,)), sems((outers,)),
        ],
        compiler_params=pltpu.CompilerParams(
            collective_id=0, has_side_effects=True, vmem_limit_bytes=VMEM_LIMIT
        ),
        name="attention_backward",
    )(
        key_rot[0], value_rows[0], segments, query_rot[0], grad_out[0], attention_out[0],
        log_norm.reshape(GROUP, 1, tokens), jnp.asarray(rotary(np.arange(tokens))),
        jnp.asarray(rotary(np.arange(inners) * tokens)),
    )
    outs = pl.pallas_call(
        write,
        out_shape=shapes,
        in_specs=[hbm] * 4,
        out_specs=(hbm,) * 4,
        scratch_shapes=[pltpu.VMEM(shape.shape, shape.dtype) for shape in shapes] + [sems((8,))],
        compiler_params=pltpu.CompilerParams(vmem_limit_bytes=VMEM_LIMIT),
        name="write_results",
    )(*outs)
    return outs[0][None], outs[1][None], outs[2][None], outs[3].reshape(-1)


def solution(mesh):
    placed = (
        P("outer", "inner", None),
        P("outer", "inner", None),
        P("outer", "inner", None),
        P("outer", "inner", None),
        P("outer", "inner", None),
        P("outer", None, "inner"),
        P(None, "inner"),
        P(None, "inner", None),
    )
    return jax.shard_map(
        functools.partial(local, mesh.shape["inner"], mesh.shape["outer"]),
        mesh=mesh,
        in_specs=placed,
        out_specs=(
            P("outer", "inner", None),
            P("outer", "inner", None),
            P("outer", "inner", None),
            P(),
        ),
        check_vma=False,
    )
```

```python
import functools
import math

import jax
import jax.numpy as jnp
import numpy as np
from jax import lax
from jax.experimental import pallas as pl
from jax.experimental.pallas import tpu as pltpu
from jax.sharding import PartitionSpec as P

HEADS = 28
KV_HEADS = 4
HEAD_DIM = 128
GROUP = HEADS // KV_HEADS
ROPE_BASE = 1000000.0
ROOT = math.sqrt(HEAD_DIM)
SCALE = 1.0 / ROOT
MASKED = -1e30
EXTRA = 16
BIAS_ROWS = 16
VMEM_LIMIT = 63 * 1024 * 1024
MESH = pl.DeviceIdType.MESH
F32 = jnp.float32
BF16 = jnp.bfloat16


def partner(index, step, count):
    result = 0
    bit = 1
    while bit < count:
        result = result + ((index // bit + step // bit) % 2) * bit
        bit *= 2
    return result


def pieces(x):
    high = x.astype(BF16).astype(F32)
    rest = x - high
    middle = rest.astype(BF16).astype(F32)
    return high, middle, rest - middle


def dot(a, b):
    return jnp.dot(a, b, preferred_element_type=F32)


def kernel(
    inners, outers, k_hbm, v_hbm, seg_hbm, q_hbm, go_hbm, ao_hbm, norm_hbm, base_hbm, starts_hbm,
    dq_hbm, dk_hbm, dv_hbm, bias_hbm,
    k_ref, v_ref, seg_ref, q_ref, go_ref, ao_ref, norm_ref, base_ref, starts_ref, load_sem,
    dq_ref, dk_ref, dv_ref, bias_ref, store_sem,
    kv, q_aug, go_aug, q_t, go_t, probs, grads, scores, pulls, keys, dq_acc, own_acc, kept, pair_out, pair_in,
    part_out, part_in,
    prob_sums, angles, bias_own, bias_in, plane_own, plane_in,
    kv_send, kv_recv, pair_send, pair_recv, part_send, part_recv, bias_send, bias_recv, plane_send, plane_recv,
):
    tokens = k_ref.shape[0]
    rows = GROUP * tokens
    me = lax.axis_index("inner")
    plane = lax.axis_index("outer")

    loads = [
        pltpu.make_async_copy(source, target, load_sem.at[i])
        for i, (source, target) in enumerate([
            (k_hbm, k_ref), (v_hbm, v_ref), (seg_hbm, seg_ref), (q_hbm, q_ref), (go_hbm, go_ref),
            (ao_hbm, ao_ref), (norm_hbm, norm_ref), (base_hbm, base_ref), (starts_hbm, starts_ref),
        ])
    ]
    for load in loads:
        load.start()
    stores = [
        pltpu.make_async_copy(source, target, store_sem.at[i])
        for i, (source, target) in enumerate([
            (dq_ref, dq_hbm), (dk_ref, dk_hbm), (dv_ref, dv_hbm), (bias_ref, bias_hbm),
        ])
    ]

    def inner_id(step):
        return (plane, partner(me, step, inners))

    def outer_id(step):
        return (partner(plane, step, outers), me)

    barrier = pltpu.get_barrier_semaphore()
    for step in range(1, inners):
        pl.semaphore_signal(barrier, inc=1, device_id=inner_id(step), device_id_type=MESH)
    for step in range(1, outers):
        pl.semaphore_signal(barrier, inc=1, device_id=outer_id(step), device_id_type=MESH)

    for load in loads[:3]:
        load.wait()
    seg = seg_ref[...].astype(F32)
    row = lax.broadcasted_iota(jnp.int32, (EXTRA, tokens), 0)
    seg_rows = jnp.broadcast_to(seg, (EXTRA, tokens))
    extra = jnp.where(row < 3, 1.0, 0.0)
    extra = jnp.where((row == 3) & (seg_rows == 1.0), 1.0, extra)
    extra = jnp.where((row == 4) & (seg_rows == 2.0), 1.0, extra)
    kv[0, :HEAD_DIM] = jnp.transpose(v_ref[...])
    kv[0, HEAD_DIM : 2 * HEAD_DIM] = jnp.transpose(k_ref[...])
    kv[0, 2 * HEAD_DIM : 2 * HEAD_DIM + EXTRA] = extra.astype(BF16)
    for slot in range(inners):
        kv[slot, 2 * HEAD_DIM + EXTRA :] = jnp.zeros((HEAD_DIM - EXTRA, tokens), BF16)

    pl.semaphore_wait(barrier, inners + outers - 2)

    sent = 2 * HEAD_DIM + EXTRA

    def kv_copy(step):
        return pltpu.make_async_remote_copy(
            src_ref=kv.at[0, pl.ds(0, sent)],
            dst_ref=kv.at[step, pl.ds(0, sent)],
            send_sem=kv_send.at[step],
            recv_sem=kv_recv.at[step],
            device_id=inner_id(step),
            device_id_type=MESH,
        )

    def forward(step):
        return pltpu.make_async_remote_copy(
            src_ref=kv.at[step, pl.ds(0, sent)],
            dst_ref=kv.at[step + 1, pl.ds(0, sent)],
            send_sem=kv_send.at[step + 1],
            recv_sem=kv_recv.at[step + 1],
            device_id=inner_id(1),
            device_id_type=MESH,
        )

    def pair_copy(g):
        return pltpu.make_async_remote_copy(
            src_ref=pair_out.at[g],
            dst_ref=pair_in.at[g],
            send_sem=pair_send.at[g],
            recv_sem=pair_recv.at[g],
            device_id=inner_id(1),
            device_id_type=MESH,
        )

    def part_copy(step):
        return pltpu.make_async_remote_copy(
            src_ref=part_out.at[step],
            dst_ref=part_in.at[step],
            send_sem=part_send.at[step],
            recv_sem=part_recv.at[step],
            device_id=inner_id(step),
            device_id_type=MESH,
        )

    groups = inners // 2
    direct = [1] + [2 * g for g in range(1, groups)]
    for step in direct:
        kv_copy(step).start()

    for load in loads[3:]:
        load.wait()
    row8 = lax.broadcasted_iota(jnp.int32, (8, tokens), 0)
    seg8 = jnp.broadcast_to(seg, (8, tokens))
    masks = jnp.where((row8 == 3) & (seg8 != 1.0), MASKED, 0.0)
    masks = jnp.where((row8 == 4) & (seg8 != 2.0), MASKED, masks)
    lane = lax.broadcasted_iota(jnp.int32, (tokens, HEAD_DIM), 1)
    for g in range(GROUP):
        here = slice(g * tokens, (g + 1) * tokens)
        cols = slice(g * HEAD_DIM, (g + 1) * HEAD_DIM)
        query = q_ref[:, cols]
        grad = go_ref[:, cols]
        q_aug[here, :HEAD_DIM] = query
        go_aug[here, :HEAD_DIM] = grad
        q_t[:, here] = jnp.transpose(query)
        go_t[:, here] = jnp.transpose(grad)
        high, middle, low = pieces(norm_ref[g] * -ROOT)
        top = jnp.where(row8 == 0, high, masks)
        top = jnp.where(row8 == 1, middle, top)
        top = jnp.where(row8 == 2, low, top)
        full = jnp.concatenate([top, jnp.zeros((HEAD_DIM - 8, tokens), F32)], axis=0)
        q_aug[here, HEAD_DIM:] = jnp.transpose(full).astype(BF16)
        delta = -jnp.sum(
            grad.astype(F32) * ao_ref[:, cols].astype(F32), axis=1, keepdims=True
        )
        d_high, d_middle, d_low = pieces(delta)
        side = jnp.where(lane == 0, d_high, 0.0)
        side = jnp.where(lane == 1, d_middle, side)
        side = jnp.where(lane == 2, d_low, side)
        go_aug[here, HEAD_DIM:] = side.astype(BF16)

    half = HEAD_DIM // 2
    for slot in range(inners):
        angles[slot : slot + 1] = starts_ref[pl.ds(partner(me, slot, inners), 1)]

    def both(table):
        below = lax.broadcasted_iota(jnp.int32, table.shape, 1) < half
        turned = pltpu.roll(table, half, 1)
        return jnp.where(below, turned, table), jnp.where(below, table, -turned)

    base_cos, base_sin = both(base_ref[...])
    start_cos, start_sin = both(angles[...])
    cosine = base_cos * start_cos[:1] - base_sin * start_sin[:1]
    sine = base_sin * start_cos[:1] + base_cos * start_sin[:1]
    base_turned = pltpu.roll(base_ref[...], half, 1)

    def waves(slot):
        start_cos, start_sin = both(angles[pl.ds(slot, 1)])
        return (base_ref[...] * start_cos + base_turned * start_sin).astype(BF16)

    def unrotate(x):
        return x * cosine + pltpu.roll(x, half, 1) * sine

    chunk = rows if tokens <= 128 else 256
    starts = list(range(0, rows, chunk))

    tile = 32

    def query_side(g, first):
        block = jnp.concatenate([kv[2 * g], kv[2 * g + 1]], axis=1)
        values_t = jnp.concatenate([block[:HEAD_DIM], block[2 * HEAD_DIM :]], axis=0)
        keys_t = block[HEAD_DIM:]
        for start in starts:
            here = slice(start, min(start + chunk, rows))
            scores[here] = dot(q_aug[here], keys_t)
            pulls[here] = dot(go_aug[here], values_t)
        keys[g, :, :HEAD_DIM] = jnp.transpose(block[HEAD_DIM : 2 * HEAD_DIM])
        keys[g, :tokens, HEAD_DIM:] = waves(2 * g)
        keys[g, tokens:, HEAD_DIM:] = waves(2 * g + 1)
        for start in range(0, rows, tile):
            here = slice(start, start + tile)
            chances = jnp.exp(scores[here] * SCALE)
            probs[g, here] = chances.astype(BF16)
            grads[g, here] = (chances * pulls[here]).astype(BF16)
            chance_part = chances[:, :HEAD_DIM]
            for col in range(HEAD_DIM, 2 * tokens, HEAD_DIM):
                chance_part = chance_part + chances[:, col : col + HEAD_DIM]
            if first:
                prob_sums[here] = chance_part
            else:
                prob_sums[here] += chance_part

    def key_side(g):
        return dot(q_t[...], grads[g]), dot(go_t[...], probs[g])

    def pass_on(g):
        kv_copy(2 * g).wait_recv()
        forward(2 * g).start()

    def turn(g):
        forward(2 * g).wait_recv()
        query_side(g, False)

    def give(g):
        key_part, value_part = key_side(g)
        pair_out[g, :HEAD_DIM] = key_part[:, tokens:].astype(BF16)
        pair_out[g, HEAD_DIM:] = value_part[:, tokens:].astype(BF16)
        pair_copy(g).start()
        kept[g, :HEAD_DIM] = key_part[:, :tokens]
        kept[g, HEAD_DIM:] = value_part[:, :tokens]

    def send_home(g):
        pair_copy(g).wait_recv()
        part_out[2 * g] = (kept[g] + pair_in[g].astype(F32)).astype(BF16)
        part_copy(2 * g).start()

    kv_copy(1).wait_recv()
    query_side(0, True)
    if groups == 4:
        pass_on(1)
        pass_on(3)
        turn(1)
        pass_on(2)
        turn(3)
        give(1)
        turn(2)
        send_home(1)
    else:

        def whole_turn(g, carry):
            pass_on(g)
            turn(g)
            return carry

        lax.fori_loop(1, groups, whole_turn, 0)

    every_key = jnp.concatenate([keys[g] for g in range(groups)], axis=0)
    for start in starts:
        here = slice(start, min(start + chunk, rows))
        every_grad = jnp.concatenate([grads[g, here] for g in range(groups)], axis=1)
        dq_acc[here] = dot(every_grad, every_key)
    bias_own[...] = jnp.zeros((BIAS_ROWS, HEAD_DIM), F32)
    key_bias = jnp.zeros((tokens, HEAD_DIM), F32)
    value_bias = jnp.zeros((tokens, HEAD_DIM), F32)
    for g in range(GROUP):
        here = slice(g * tokens, (g + 1) * tokens)
        cols = slice(g * HEAD_DIM, (g + 1) * HEAD_DIM)
        full = unrotate(dq_acc[here, :HEAD_DIM] * SCALE)
        dq_ref[:, cols] = full.astype(BF16)
        bias_own[g : g + 1] = jnp.sum(full, axis=0, keepdims=True)
        query = q_ref[:, cols].astype(F32)
        turn_cos, turn_sin = both(dq_acc[here, HEAD_DIM:])
        key_bias = key_bias + query * turn_cos + pltpu.roll(query, half, 1) * turn_sin
        weight = jnp.sum(prob_sums[here], axis=1, keepdims=True)
        value_bias = value_bias + weight * go_ref[:, cols].astype(F32)
    bias_own[GROUP : GROUP + 1] = jnp.sum(key_bias, axis=0, keepdims=True) * SCALE
    bias_own[GROUP + 1 : GROUP + 2] = jnp.sum(value_bias, axis=0, keepdims=True)

    def bias_copy(step, slot):
        return pltpu.make_async_remote_copy(
            src_ref=bias_own,
            dst_ref=bias_in.at[slot],
            send_sem=bias_send.at[step],
            recv_sem=bias_recv.at[step],
            device_id=inner_id(step),
            device_id_type=MESH,
        )

    def plane_copy(step, slot):
        return pltpu.make_async_remote_copy(
            src_ref=plane_own,
            dst_ref=plane_in.at[slot],
            send_sem=plane_send.at[step],
            recv_sem=plane_recv.at[step],
            device_id=outer_id(step),
            device_id_type=MESH,
        )

    def bias_along():
        for step in range(1, inners):
            bias_copy(step, partner(me, step, inners)).wait_recv()
        summed = bias_in[0]
        for slot in range(1, inners):
            summed = summed + bias_in[slot]
        plane_own[...] = summed
        for step in range(1, outers):
            plane_copy(step, plane).start()
        plane_in[plane] = summed

    for step in range(1, inners):
        bias_copy(step, me).start()
    stores[0].start()
    bias_in[me] = bias_own[...]
    if groups == 4:
        give(3)
        give(2)
        send_home(3)
        bias_along()
    else:

        def whole_give(g, carry):
            give(g)
            send_home(g)
            return carry

        lax.fori_loop(1, groups, whole_give, 0)
        bias_along()
    key_part, value_part = key_side(0)
    part_out[1, :HEAD_DIM] = key_part[:, tokens:].astype(BF16)
    part_out[1, HEAD_DIM:] = value_part[:, tokens:].astype(BF16)
    part_copy(1).start()
    if groups == 4:
        send_home(2)
    own_acc[:HEAD_DIM] = key_part[:, :tokens]
    own_acc[HEAD_DIM:] = value_part[:, :tokens]

    total = own_acc[...]
    for step in direct:
        part_copy(step).wait_recv()
        total = total + part_in[step].astype(F32)
    key_full = unrotate(jnp.transpose(total[:HEAD_DIM]) * SCALE)
    value_full = jnp.transpose(total[HEAD_DIM:])
    dk_ref[...] = key_full.astype(BF16)
    dv_ref[...] = value_full.astype(BF16)
    stores[1].start()
    stores[2].start()

    for step in range(1, outers):
        plane_copy(step, partner(plane, step, outers)).wait_recv()
    for head in range(KV_HEADS):
        whole = plane_in[head]
        for other in range(head + KV_HEADS, outers, KV_HEADS):
            whole = whole + plane_in[other]
        bias_ref[head * GROUP : (head + 1) * GROUP] = whole[:GROUP]
        bias_ref[HEADS + head : HEADS + head + 1] = whole[GROUP : GROUP + 1]
        at = HEADS + KV_HEADS + head
        bias_ref[at : at + 1] = whole[GROUP + 1 : GROUP + 2]
    stores[3].start()

    for step in direct:
        kv_copy(step).wait_send()
        part_copy(step).wait_send()
    for g in range(1, groups):
        forward(2 * g).wait_send()
        pair_copy(g).wait_send()
    for step in range(1, inners):
        bias_copy(step, me).wait_send()
    for step in range(1, outers):
        plane_copy(step, plane).wait_send()
    for store in stores:
        store.wait()


def write(*refs):
    sources, targets, held, sem = refs[:4], refs[4:8], refs[8:12], refs[12]
    loads = [pltpu.make_async_copy(sources[i], held[i], sem.at[i]) for i in range(4)]
    stores = [pltpu.make_async_copy(held[i], targets[i], sem.at[4 + i]) for i in range(4)]
    for load in loads:
        load.start()
    for load, store in zip(loads, stores):
        load.wait()
        store.start()
    for store in stores:
        store.wait()


def rotary(positions):
    frequency = np.exp(np.arange(HEAD_DIM // 2) * (-2.0 * math.log(ROPE_BASE) / HEAD_DIM))
    angles = np.asarray(positions)[:, None] * frequency[None, :]
    return np.concatenate([np.sin(angles), np.cos(angles)], axis=1).astype(np.float32)


def local(inners, outers, query_rot, key_rot, value_rows, attention_out, grad_out, log_norm,
          segments, block_table):
    del block_table
    tokens = query_rot.shape[1]
    rows = GROUP * tokens
    if segments.shape[0] > 1:
        example = lax.axis_index("outer") // KV_HEADS
        segments = lax.dynamic_slice_in_dim(segments, example, 1, 0)
    hbm = pl.BlockSpec(memory_space=pltpu.HBM)
    sems = pltpu.SemaphoreType.DMA
    shapes = (
        jax.ShapeDtypeStruct((tokens, GROUP * HEAD_DIM), BF16),
        jax.ShapeDtypeStruct((tokens, HEAD_DIM), BF16),
        jax.ShapeDtypeStruct((tokens, HEAD_DIM), BF16),
        jax.ShapeDtypeStruct((HEADS + 2 * KV_HEADS, HEAD_DIM), F32),
    )
    outs = pl.pallas_call(
        functools.partial(kernel, inners, outers),
        out_shape=shapes,
        in_specs=[hbm] * 9,
        out_specs=(hbm,) * 4,
        scratch_shapes=[
            pltpu.VMEM((tokens, HEAD_DIM), BF16),
            pltpu.VMEM((tokens, HEAD_DIM), BF16),
            pltpu.VMEM((1, tokens), jnp.int32),
            pltpu.VMEM((tokens, GROUP * HEAD_DIM), BF16),
            pltpu.VMEM((tokens, GROUP * HEAD_DIM), BF16),
            pltpu.VMEM((tokens, GROUP * HEAD_DIM), BF16),
            pltpu.VMEM((GROUP, 1, tokens), F32),
            pltpu.VMEM((tokens, HEAD_DIM), F32),
            pltpu.VMEM((inners, HEAD_DIM), F32),
            sems((9,)),
            pltpu.VMEM((tokens, GROUP * HEAD_DIM), BF16),
            pltpu.VMEM((tokens, HEAD_DIM), BF16),
            pltpu.VMEM((tokens, HEAD_DIM), BF16),
            pltpu.VMEM((HEADS + 2 * KV_HEADS, HEAD_DIM), F32),
            sems((4,)),
            pltpu.VMEM((inners, 3 * HEAD_DIM, tokens), BF16),
            pltpu.VMEM((rows, 2 * HEAD_DIM), BF16),
            pltpu.VMEM((rows, 2 * HEAD_DIM), BF16),
            pltpu.VMEM((HEAD_DIM, rows), BF16),
            pltpu.VMEM((HEAD_DIM, rows), BF16),
            pltpu.VMEM((inners // 2, rows, 2 * tokens), BF16),
            pltpu.VMEM((inners // 2, rows, 2 * tokens), BF16),
            pltpu.VMEM((rows, 2 * tokens), F32),
            pltpu.VMEM((rows, 2 * tokens), F32),
            pltpu.VMEM((inners // 2, 2 * tokens, 2 * HEAD_DIM), BF16),
            pltpu.VMEM((rows, 2 * HEAD_DIM), F32),
            pltpu.VMEM((2 * HEAD_DIM, tokens), F32),
            pltpu.VMEM((inners // 2, 2 * HEAD_DIM, tokens), F32),
            pltpu.VMEM((inners // 2, 2 * HEAD_DIM, tokens), BF16),
            pltpu.VMEM((inners // 2, 2 * HEAD_DIM, tokens), BF16),
            pltpu.VMEM((inners, 2 * HEAD_DIM, tokens), BF16),
            pltpu.VMEM((inners, 2 * HEAD_DIM, tokens), BF16),
            pltpu.VMEM((rows, HEAD_DIM), F32),
            pltpu.VMEM((inners, HEAD_DIM), F32),
            pltpu.VMEM((BIAS_ROWS, HEAD_DIM), F32),
            pltpu.VMEM((inners, BIAS_ROWS, HEAD_DIM), F32),
            pltpu.VMEM((BIAS_ROWS, HEAD_DIM), F32),
            pltpu.VMEM((outers, BIAS_ROWS, HEAD_DIM), F32),
            sems((inners,)), sems((inners,)), sems((inners // 2,)), sems((inners // 2,)),
            sems((inners,)), sems((inners,)),
            sems((inners,)), sems((inners,)), sems((outers,)), sems((outers,)),
        ],
        compiler_params=pltpu.CompilerParams(
            collective_id=0, has_side_effects=True, vmem_limit_bytes=VMEM_LIMIT
        ),
        name="attention_backward",
    )(
        key_rot[0], value_rows[0], segments, query_rot[0], grad_out[0], attention_out[0],
        log_norm.reshape(GROUP, 1, tokens), jnp.asarray(rotary(np.arange(tokens))),
        jnp.asarray(rotary(np.arange(inners) * tokens)),
    )
    outs = pl.pallas_call(
        write,
        out_shape=shapes,
        in_specs=[hbm] * 4,
        out_specs=(hbm,) * 4,
        scratch_shapes=[pltpu.VMEM(shape.shape, shape.dtype) for shape in shapes] + [sems((8,))],
        compiler_params=pltpu.CompilerParams(vmem_limit_bytes=VMEM_LIMIT),
        name="write_results",
    )(*outs)
    return outs[0][None], outs[1][None], outs[2][None], outs[3].reshape(-1)


def solution(mesh):
    placed = (
        P("outer", "inner", None),
        P("outer", "inner", None),
        P("outer", "inner", None),
        P("outer", "inner", None),
        P("outer", "inner", None),
        P("outer", None, "inner"),
        P(None, "inner"),
        P(None, "inner", None),
    )
    return jax.shard_map(
        functools.partial(local, mesh.shape["inner"], mesh.shape["outer"]),
        mesh=mesh,
        in_specs=placed,
        out_specs=(
            P("outer", "inner", None),
            P("outer", "inner", None),
            P("outer", "inner", None),
            P(),
        ),
        check_vma=False,
    )
```

```python
import functools
import math

import jax
import jax.numpy as jnp
import numpy as np
from jax import lax
from jax.experimental import pallas as pl
from jax.experimental.pallas import tpu as pltpu
from jax.sharding import PartitionSpec as P

HEADS = 28
KV_HEADS = 4
HEAD_DIM = 128
GROUP = HEADS // KV_HEADS
ROPE_BASE = 1000000.0
ROOT = math.sqrt(HEAD_DIM)
SCALE = 1.0 / ROOT
MASKED = -1e30
EXTRA = 16
BIAS_ROWS = 16
VMEM_LIMIT = 63 * 1024 * 1024
MESH = pl.DeviceIdType.MESH
F32 = jnp.float32
BF16 = jnp.bfloat16


def partner(index, step, count):
    result = 0
    bit = 1
    while bit < count:
        result = result + ((index // bit + step // bit) % 2) * bit
        bit *= 2
    return result


def pieces(x):
    high = x.astype(BF16).astype(F32)
    rest = x - high
    middle = rest.astype(BF16).astype(F32)
    return high, middle, rest - middle


def dot(a, b):
    return jnp.dot(a, b, preferred_element_type=F32)


def kernel(
    inners, outers, k_hbm, v_hbm, seg_hbm, q_hbm, go_hbm, ao_hbm, norm_hbm, base_hbm, starts_hbm,
    dq_hbm, dk_hbm, dv_hbm, bias_hbm,
    k_ref, v_ref, seg_ref, q_ref, go_ref, ao_ref, norm_ref, base_ref, starts_ref, load_sem,
    dq_ref, dk_ref, dv_ref, bias_ref, store_sem,
    kv, q_aug, go_aug, q_t, go_t, probs, grads, scores, pulls, keys, dq_acc, own_acc, kept, pair_out, pair_in,
    part_out, part_in,
    prob_sums, angles, bias_own, bias_in, plane_own, plane_in,
    kv_send, kv_recv, pair_send, pair_recv, part_send, part_recv, bias_send, bias_recv, plane_send, plane_recv,
):
    tokens = k_ref.shape[0]
    rows = GROUP * tokens
    me = lax.axis_index("inner")
    plane = lax.axis_index("outer")

    loads = [
        pltpu.make_async_copy(source, target, load_sem.at[i])
        for i, (source, target) in enumerate([
            (k_hbm, k_ref), (v_hbm, v_ref), (seg_hbm, seg_ref), (q_hbm, q_ref), (go_hbm, go_ref),
            (ao_hbm, ao_ref), (norm_hbm, norm_ref), (base_hbm, base_ref), (starts_hbm, starts_ref),
        ])
    ]
    for load in loads:
        load.start()
    stores = [
        pltpu.make_async_copy(source, target, store_sem.at[i])
        for i, (source, target) in enumerate([
            (dq_ref, dq_hbm), (dk_ref, dk_hbm), (dv_ref, dv_hbm), (bias_ref, bias_hbm),
        ])
    ]

    def inner_id(step):
        return (plane, partner(me, step, inners))

    def outer_id(step):
        return (partner(plane, step, outers), me)

    barrier = pltpu.get_barrier_semaphore()
    for step in range(1, inners):
        pl.semaphore_signal(barrier, inc=1, device_id=inner_id(step), device_id_type=MESH)
    for step in range(1, outers):
        pl.semaphore_signal(barrier, inc=1, device_id=outer_id(step), device_id_type=MESH)

    for load in loads[:3]:
        load.wait()
    seg = seg_ref[...].astype(F32)
    row = lax.broadcasted_iota(jnp.int32, (EXTRA, tokens), 0)
    seg_rows = jnp.broadcast_to(seg, (EXTRA, tokens))
    extra = jnp.where(row < 3, 1.0, 0.0)
    extra = jnp.where((row == 3) & (seg_rows == 1.0), 1.0, extra)
    extra = jnp.where((row == 4) & (seg_rows == 2.0), 1.0, extra)
    kv[0, :HEAD_DIM] = jnp.transpose(v_ref[...])
    kv[0, HEAD_DIM : 2 * HEAD_DIM] = jnp.transpose(k_ref[...])
    kv[0, 2 * HEAD_DIM : 2 * HEAD_DIM + EXTRA] = extra.astype(BF16)
    for slot in range(inners):
        kv[slot, 2 * HEAD_DIM + EXTRA :] = jnp.zeros((HEAD_DIM - EXTRA, tokens), BF16)

    sent = 2 * HEAD_DIM + EXTRA

    def kv_copy(step):
        return pltpu.make_async_remote_copy(
            src_ref=kv.at[0, pl.ds(0, sent)],
            dst_ref=kv.at[step, pl.ds(0, sent)],
            send_sem=kv_send.at[step],
            recv_sem=kv_recv.at[step],
            device_id=inner_id(step),
            device_id_type=MESH,
        )

    def forward(step):
        return pltpu.make_async_remote_copy(
            src_ref=kv.at[step, pl.ds(0, sent)],
            dst_ref=kv.at[step + 1, pl.ds(0, sent)],
            send_sem=kv_send.at[step + 1],
            recv_sem=kv_recv.at[step + 1],
            device_id=inner_id(1),
            device_id_type=MESH,
        )

    def pair_copy(g):
        return pltpu.make_async_remote_copy(
            src_ref=pair_out.at[g],
            dst_ref=pair_in.at[g],
            send_sem=pair_send.at[g],
            recv_sem=pair_recv.at[g],
            device_id=inner_id(1),
            device_id_type=MESH,
        )

    def part_copy(step):
        return pltpu.make_async_remote_copy(
            src_ref=part_out.at[step],
            dst_ref=part_in.at[step],
            send_sem=part_send.at[step],
            recv_sem=part_recv.at[step],
            device_id=inner_id(step),
            device_id_type=MESH,
        )

    groups = inners // 2
    direct = [1] + [2 * g for g in range(1, groups)]
    for load in loads[3:]:
        load.wait()
    row8 = lax.broadcasted_iota(jnp.int32, (8, tokens), 0)
    seg8 = jnp.broadcast_to(seg, (8, tokens))
    masks = jnp.where((row8 == 3) & (seg8 != 1.0), MASKED, 0.0)
    masks = jnp.where((row8 == 4) & (seg8 != 2.0), MASKED, masks)
    lane = lax.broadcasted_iota(jnp.int32, (tokens, HEAD_DIM), 1)
    for g in range(GROUP):
        here = slice(g * tokens, (g + 1) * tokens)
        cols = slice(g * HEAD_DIM, (g + 1) * HEAD_DIM)
        query = q_ref[:, cols]
        grad = go_ref[:, cols]
        q_aug[here, :HEAD_DIM] = query
        go_aug[here, :HEAD_DIM] = grad
        high, middle, low = pieces(norm_ref[g] * -ROOT)
        top = jnp.where(row8 == 0, high, masks)
        top = jnp.where(row8 == 1, middle, top)
        top = jnp.where(row8 == 2, low, top)
        full = jnp.concatenate([top, jnp.zeros((HEAD_DIM - 8, tokens), F32)], axis=0)
        q_aug[here, HEAD_DIM:] = jnp.transpose(full).astype(BF16)
        delta = -jnp.sum(
            grad.astype(F32) * ao_ref[:, cols].astype(F32), axis=1, keepdims=True
        )
        d_high, d_middle, d_low = pieces(delta)
        side = jnp.where(lane == 0, d_high, 0.0)
        side = jnp.where(lane == 1, d_middle, side)
        side = jnp.where(lane == 2, d_low, side)
        go_aug[here, HEAD_DIM:] = side.astype(BF16)

    half = HEAD_DIM // 2
    for slot in range(inners):
        angles[slot : slot + 1] = starts_ref[pl.ds(partner(me, slot, inners), 1)]

    def both(table):
        below = lax.broadcasted_iota(jnp.int32, table.shape, 1) < half
        turned = pltpu.roll(table, half, 1)
        return jnp.where(below, turned, table), jnp.where(below, table, -turned)

    base_cos, base_sin = both(base_ref[...])
    start_cos, start_sin = both(angles[...])
    cosine = base_cos * start_cos[:1] - base_sin * start_sin[:1]
    sine = base_sin * start_cos[:1] + base_cos * start_sin[:1]
    base_turned = pltpu.roll(base_ref[...], half, 1)

    def waves(slot):
        start_cos, start_sin = both(angles[pl.ds(slot, 1)])
        return (base_ref[...] * start_cos + base_turned * start_sin).astype(BF16)

    def unrotate(x):
        return x * cosine + pltpu.roll(x, half, 1) * sine

    chunk = rows if tokens <= 128 else 256
    starts = list(range(0, rows, chunk))

    tile = 32

    def query_side(g, first):
        block = jnp.concatenate([kv[2 * g], kv[2 * g + 1]], axis=1)
        values_t = jnp.concatenate([block[:HEAD_DIM], block[2 * HEAD_DIM :]], axis=0)
        keys_t = block[HEAD_DIM:]
        for start in starts:
            here = slice(start, min(start + chunk, rows))
            scores[here] = dot(q_aug[here], keys_t)
            pulls[here] = dot(go_aug[here], values_t)
        keys[g, :, :HEAD_DIM] = jnp.transpose(block[HEAD_DIM : 2 * HEAD_DIM])
        keys[g, :tokens, HEAD_DIM:] = waves(2 * g)
        keys[g, tokens:, HEAD_DIM:] = waves(2 * g + 1)
        for start in range(0, rows, tile):
            here = slice(start, start + tile)
            chances = jnp.exp(scores[here] * SCALE)
            probs[g, here] = chances.astype(BF16)
            grads[g, here] = (chances * pulls[here]).astype(BF16)
            chance_part = chances[:, :HEAD_DIM]
            for col in range(HEAD_DIM, 2 * tokens, HEAD_DIM):
                chance_part = chance_part + chances[:, col : col + HEAD_DIM]
            if first:
                prob_sums[here] = chance_part
            else:
                prob_sums[here] += chance_part

    def key_side(g):
        return dot(q_t[...], grads[g]), dot(go_t[...], probs[g])

    def turn_over():
        for g in range(GROUP):
            here = slice(g * tokens, (g + 1) * tokens)
            cols = slice(g * HEAD_DIM, (g + 1) * HEAD_DIM)
            q_t[:, here] = jnp.transpose(q_ref[:, cols])
            go_t[:, here] = jnp.transpose(go_ref[:, cols])

    def pass_on(g):
        kv_copy(2 * g).wait_recv()
        forward(2 * g).start()

    def turn(g):
        forward(2 * g).wait_recv()
        query_side(g, False)

    def give(g):
        key_part, value_part = key_side(g)
        pair_out[g, :HEAD_DIM] = key_part[:, tokens:].astype(BF16)
        pair_out[g, HEAD_DIM:] = value_part[:, tokens:].astype(BF16)
        pair_copy(g).start()
        kept[g, :HEAD_DIM] = key_part[:, :tokens]
        kept[g, HEAD_DIM:] = value_part[:, :tokens]

    def send_home(g):
        pair_copy(g).wait_recv()
        part_out[2 * g] = (kept[g] + pair_in[g].astype(F32)).astype(BF16)
        part_copy(2 * g).start()

    pl.semaphore_wait(barrier, inners + outers - 2)
    for step in direct:
        kv_copy(step).start()

    kv_copy(1).wait_recv()
    query_side(0, True)
    if groups == 4:
        pass_on(1)
        pass_on(3)
        turn_over()
        turn(1)
        pass_on(2)
        turn(3)
        give(1)
        turn(2)
        send_home(1)
    else:
        turn_over()

        def whole_turn(g, carry):
            pass_on(g)
            turn(g)
            return carry

        lax.fori_loop(1, groups, whole_turn, 0)

    every_key = jnp.concatenate([keys[g] for g in range(groups)], axis=0)
    for start in starts:
        here = slice(start, min(start + chunk, rows))
        every_grad = jnp.concatenate([grads[g, here] for g in range(groups)], axis=1)
        dq_acc[here] = dot(every_grad, every_key)
    bias_own[...] = jnp.zeros((BIAS_ROWS, HEAD_DIM), F32)
    key_bias = jnp.zeros((tokens, HEAD_DIM), F32)
    value_bias = jnp.zeros((tokens, HEAD_DIM), F32)
    for g in range(GROUP):
        here = slice(g * tokens, (g + 1) * tokens)
        cols = slice(g * HEAD_DIM, (g + 1) * HEAD_DIM)
        full = unrotate(dq_acc[here, :HEAD_DIM] * SCALE)
        dq_ref[:, cols] = full.astype(BF16)
        bias_own[g : g + 1] = jnp.sum(full, axis=0, keepdims=True)
        query = q_ref[:, cols].astype(F32)
        turn_cos, turn_sin = both(dq_acc[here, HEAD_DIM:])
        key_bias = key_bias + query * turn_cos + pltpu.roll(query, half, 1) * turn_sin
        weight = jnp.sum(prob_sums[here], axis=1, keepdims=True)
        value_bias = value_bias + weight * go_ref[:, cols].astype(F32)
    bias_own[GROUP : GROUP + 1] = jnp.sum(key_bias, axis=0, keepdims=True) * SCALE
    bias_own[GROUP + 1 : GROUP + 2] = jnp.sum(value_bias, axis=0, keepdims=True)

    def bias_copy(step, slot):
        return pltpu.make_async_remote_copy(
            src_ref=bias_own,
            dst_ref=bias_in.at[slot],
            send_sem=bias_send.at[step],
            recv_sem=bias_recv.at[step],
            device_id=inner_id(step),
            device_id_type=MESH,
        )

    def plane_copy(step, slot):
        return pltpu.make_async_remote_copy(
            src_ref=plane_own,
            dst_ref=plane_in.at[slot],
            send_sem=plane_send.at[step],
            recv_sem=plane_recv.at[step],
            device_id=outer_id(step),
            device_id_type=MESH,
        )

    def bias_along():
        for step in range(1, inners):
            bias_copy(step, partner(me, step, inners)).wait_recv()
        summed = bias_in[0]
        for slot in range(1, inners):
            summed = summed + bias_in[slot]
        plane_own[...] = summed
        for step in range(1, outers):
            plane_copy(step, plane).start()
        plane_in[plane] = summed

    for step in range(1, inners):
        bias_copy(step, me).start()
    stores[0].start()
    bias_in[me] = bias_own[...]
    if groups == 4:
        give(3)
        give(2)
        send_home(3)
        bias_along()
    else:

        def whole_give(g, carry):
            give(g)
            send_home(g)
            return carry

        lax.fori_loop(1, groups, whole_give, 0)
        bias_along()
    key_part, value_part = key_side(0)
    part_out[1, :HEAD_DIM] = key_part[:, tokens:].astype(BF16)
    part_out[1, HEAD_DIM:] = value_part[:, tokens:].astype(BF16)
    part_copy(1).start()
    if groups == 4:
        send_home(2)
    own_acc[:HEAD_DIM] = key_part[:, :tokens]
    own_acc[HEAD_DIM:] = value_part[:, :tokens]

    total = own_acc[...]
    for step in direct:
        part_copy(step).wait_recv()
        total = total + part_in[step].astype(F32)
    key_full = unrotate(jnp.transpose(total[:HEAD_DIM]) * SCALE)
    value_full = jnp.transpose(total[HEAD_DIM:])
    dk_ref[...] = key_full.astype(BF16)
    dv_ref[...] = value_full.astype(BF16)
    stores[1].start()
    stores[2].start()

    for step in range(1, outers):
        plane_copy(step, partner(plane, step, outers)).wait_recv()
    for head in range(KV_HEADS):
        whole = plane_in[head]
        for other in range(head + KV_HEADS, outers, KV_HEADS):
            whole = whole + plane_in[other]
        bias_ref[head * GROUP : (head + 1) * GROUP] = whole[:GROUP]
        bias_ref[HEADS + head : HEADS + head + 1] = whole[GROUP : GROUP + 1]
        at = HEADS + KV_HEADS + head
        bias_ref[at : at + 1] = whole[GROUP + 1 : GROUP + 2]
    stores[3].start()

    for step in direct:
        kv_copy(step).wait_send()
        part_copy(step).wait_send()
    for g in range(1, groups):
        forward(2 * g).wait_send()
        pair_copy(g).wait_send()
    for step in range(1, inners):
        bias_copy(step, me).wait_send()
    for step in range(1, outers):
        plane_copy(step, plane).wait_send()
    for store in stores:
        store.wait()


def write(*refs):
    sources, targets, held, sem = refs[:4], refs[4:8], refs[8:12], refs[12]
    loads = [pltpu.make_async_copy(sources[i], held[i], sem.at[i]) for i in range(4)]
    stores = [pltpu.make_async_copy(held[i], targets[i], sem.at[4 + i]) for i in range(4)]
    for load in loads:
        load.start()
    for load, store in zip(loads, stores):
        load.wait()
        store.start()
    for store in stores:
        store.wait()


def rotary(positions):
    frequency = np.exp(np.arange(HEAD_DIM // 2) * (-2.0 * math.log(ROPE_BASE) / HEAD_DIM))
    angles = np.asarray(positions)[:, None] * frequency[None, :]
    return np.concatenate([np.sin(angles), np.cos(angles)], axis=1).astype(np.float32)


def local(inners, outers, query_rot, key_rot, value_rows, attention_out, grad_out, log_norm,
          segments, block_table):
    del block_table
    tokens = query_rot.shape[1]
    rows = GROUP * tokens
    if segments.shape[0] > 1:
        example = lax.axis_index("outer") // KV_HEADS
        segments = lax.dynamic_slice_in_dim(segments, example, 1, 0)
    hbm = pl.BlockSpec(memory_space=pltpu.HBM)
    sems = pltpu.SemaphoreType.DMA
    shapes = (
        jax.ShapeDtypeStruct((tokens, GROUP * HEAD_DIM), BF16),
        jax.ShapeDtypeStruct((tokens, HEAD_DIM), BF16),
        jax.ShapeDtypeStruct((tokens, HEAD_DIM), BF16),
        jax.ShapeDtypeStruct((HEADS + 2 * KV_HEADS, HEAD_DIM), F32),
    )
    outs = pl.pallas_call(
        functools.partial(kernel, inners, outers),
        out_shape=shapes,
        in_specs=[hbm] * 9,
        out_specs=(hbm,) * 4,
        scratch_shapes=[
            pltpu.VMEM((tokens, HEAD_DIM), BF16),
            pltpu.VMEM((tokens, HEAD_DIM), BF16),
            pltpu.VMEM((1, tokens), jnp.int32),
            pltpu.VMEM((tokens, GROUP * HEAD_DIM), BF16),
            pltpu.VMEM((tokens, GROUP * HEAD_DIM), BF16),
            pltpu.VMEM((tokens, GROUP * HEAD_DIM), BF16),
            pltpu.VMEM((GROUP, 1, tokens), F32),
            pltpu.VMEM((tokens, HEAD_DIM), F32),
            pltpu.VMEM((inners, HEAD_DIM), F32),
            sems((9,)),
            pltpu.VMEM((tokens, GROUP * HEAD_DIM), BF16),
            pltpu.VMEM((tokens, HEAD_DIM), BF16),
            pltpu.VMEM((tokens, HEAD_DIM), BF16),
            pltpu.VMEM((HEADS + 2 * KV_HEADS, HEAD_DIM), F32),
            sems((4,)),
            pltpu.VMEM((inners, 3 * HEAD_DIM, tokens), BF16),
            pltpu.VMEM((rows, 2 * HEAD_DIM), BF16),
            pltpu.VMEM((rows, 2 * HEAD_DIM), BF16),
            pltpu.VMEM((HEAD_DIM, rows), BF16),
            pltpu.VMEM((HEAD_DIM, rows), BF16),
            pltpu.VMEM((inners // 2, rows, 2 * tokens), BF16),
            pltpu.VMEM((inners // 2, rows, 2 * tokens), BF16),
            pltpu.VMEM((rows, 2 * tokens), F32),
            pltpu.VMEM((rows, 2 * tokens), F32),
            pltpu.VMEM((inners // 2, 2 * tokens, 2 * HEAD_DIM), BF16),
            pltpu.VMEM((rows, 2 * HEAD_DIM), F32),
            pltpu.VMEM((2 * HEAD_DIM, tokens), F32),
            pltpu.VMEM((inners // 2, 2 * HEAD_DIM, tokens), F32),
            pltpu.VMEM((inners // 2, 2 * HEAD_DIM, tokens), BF16),
            pltpu.VMEM((inners // 2, 2 * HEAD_DIM, tokens), BF16),
            pltpu.VMEM((inners, 2 * HEAD_DIM, tokens), BF16),
            pltpu.VMEM((inners, 2 * HEAD_DIM, tokens), BF16),
            pltpu.VMEM((rows, HEAD_DIM), F32),
            pltpu.VMEM((inners, HEAD_DIM), F32),
            pltpu.VMEM((BIAS_ROWS, HEAD_DIM), F32),
            pltpu.VMEM((inners, BIAS_ROWS, HEAD_DIM), F32),
            pltpu.VMEM((BIAS_ROWS, HEAD_DIM), F32),
            pltpu.VMEM((outers, BIAS_ROWS, HEAD_DIM), F32),
            sems((inners,)), sems((inners,)), sems((inners // 2,)), sems((inners // 2,)),
            sems((inners,)), sems((inners,)),
            sems((inners,)), sems((inners,)), sems((outers,)), sems((outers,)),
        ],
        compiler_params=pltpu.CompilerParams(
            collective_id=0, has_side_effects=True, vmem_limit_bytes=VMEM_LIMIT
        ),
        name="attention_backward",
    )(
        key_rot[0], value_rows[0], segments, query_rot[0], grad_out[0], attention_out[0],
        log_norm.reshape(GROUP, 1, tokens), jnp.asarray(rotary(np.arange(tokens))),
        jnp.asarray(rotary(np.arange(inners) * tokens)),
    )
    outs = pl.pallas_call(
        write,
        out_shape=shapes,
        in_specs=[hbm] * 4,
        out_specs=(hbm,) * 4,
        scratch_shapes=[pltpu.VMEM(shape.shape, shape.dtype) for shape in shapes] + [sems((8,))],
        compiler_params=pltpu.CompilerParams(vmem_limit_bytes=VMEM_LIMIT),
        name="write_results",
    )(*outs)
    return outs[0][None], outs[1][None], outs[2][None], outs[3].reshape(-1)


def solution(mesh):
    placed = (
        P("outer", "inner", None),
        P("outer", "inner", None),
        P("outer", "inner", None),
        P("outer", "inner", None),
        P("outer", "inner", None),
        P("outer", None, "inner"),
        P(None, "inner"),
        P(None, "inner", None),
    )
    return jax.shard_map(
        functools.partial(local, mesh.shape["inner"], mesh.shape["outer"]),
        mesh=mesh,
        in_specs=placed,
        out_specs=(
            P("outer", "inner", None),
            P("outer", "inner", None),
            P("outer", "inner", None),
            P(),
        ),
        check_vma=False,
    )
```

```python
import functools
import math

import jax
import jax.numpy as jnp
import numpy as np
from jax import lax
from jax.experimental import pallas as pl
from jax.experimental.pallas import tpu as pltpu
from jax.sharding import PartitionSpec as P

HEADS = 28
KV_HEADS = 4
HEAD_DIM = 128
GROUP = HEADS // KV_HEADS
ROPE_BASE = 1000000.0
ROOT = math.sqrt(HEAD_DIM)
SCALE = 1.0 / ROOT
MASKED = -1e30
EXTRA = 16
BIAS_ROWS = 16
VMEM_LIMIT = 63 * 1024 * 1024
MESH = pl.DeviceIdType.MESH
F32 = jnp.float32
BF16 = jnp.bfloat16


def partner(index, step, count):
    result = 0
    bit = 1
    while bit < count:
        result = result + ((index // bit + step // bit) % 2) * bit
        bit *= 2
    return result


def pieces(x):
    high = x.astype(BF16).astype(F32)
    rest = x - high
    middle = rest.astype(BF16).astype(F32)
    return high, middle, rest - middle


def dot(a, b):
    return jnp.dot(a, b, preferred_element_type=F32)


def kernel(
    inners, outers, k_hbm, v_hbm, seg_hbm, q_hbm, go_hbm, ao_hbm, norm_hbm, base_hbm, starts_hbm,
    dq_hbm, dk_hbm, dv_hbm, bias_hbm,
    k_ref, v_ref, seg_ref, q_ref, go_ref, ao_ref, norm_ref, base_ref, starts_ref, load_sem,
    dq_ref, dk_ref, dv_ref, bias_ref, store_sem,
    kv, q_aug, go_aug, q_t, go_t, probs, grads, scores, pulls, keys, dq_acc, own_acc, kept, pair_out, pair_in,
    part_out, part_in,
    prob_sums, angles, bias_own, bias_in, plane_own, plane_in,
    kv_send, kv_recv, pair_send, pair_recv, part_send, part_recv, bias_send, bias_recv, plane_send, plane_recv,
):
    tokens = k_ref.shape[0]
    rows = GROUP * tokens
    me = lax.axis_index("inner")
    plane = lax.axis_index("outer")

    loads = [
        pltpu.make_async_copy(source, target, load_sem.at[i])
        for i, (source, target) in enumerate([
            (k_hbm, k_ref), (v_hbm, v_ref), (seg_hbm, seg_ref), (q_hbm, q_ref), (go_hbm, go_ref),
            (ao_hbm, ao_ref), (norm_hbm, norm_ref), (base_hbm, base_ref), (starts_hbm, starts_ref),
        ])
    ]
    for load in loads:
        load.start()
    stores = [
        pltpu.make_async_copy(source, target, store_sem.at[i])
        for i, (source, target) in enumerate([
            (dq_ref, dq_hbm), (dk_ref, dk_hbm), (dv_ref, dv_hbm), (bias_ref, bias_hbm),
        ])
    ]

    def inner_id(step):
        return (plane, partner(me, step, inners))

    def outer_id(step):
        return (partner(plane, step, outers), me)

    barrier = pltpu.get_barrier_semaphore()
    for step in range(1, inners):
        pl.semaphore_signal(barrier, inc=1, device_id=inner_id(step), device_id_type=MESH)
    for step in range(1, outers):
        pl.semaphore_signal(barrier, inc=1, device_id=outer_id(step), device_id_type=MESH)

    for load in loads[:3]:
        load.wait()
    seg = seg_ref[...].astype(F32)
    row = lax.broadcasted_iota(jnp.int32, (EXTRA, tokens), 0)
    seg_rows = jnp.broadcast_to(seg, (EXTRA, tokens))
    extra = jnp.where(row < 3, 1.0, 0.0)
    extra = jnp.where((row == 3) & (seg_rows == 1.0), 1.0, extra)
    extra = jnp.where((row == 4) & (seg_rows == 2.0), 1.0, extra)
    kv[0, :HEAD_DIM] = jnp.transpose(v_ref[...])
    kv[0, HEAD_DIM : 2 * HEAD_DIM] = jnp.transpose(k_ref[...])
    kv[0, 2 * HEAD_DIM : 2 * HEAD_DIM + EXTRA] = extra.astype(BF16)
    for slot in range(inners):
        kv[slot, 2 * HEAD_DIM + EXTRA :] = jnp.zeros((HEAD_DIM - EXTRA, tokens), BF16)

    sent = 2 * HEAD_DIM + EXTRA

    def kv_copy(step):
        return pltpu.make_async_remote_copy(
            src_ref=kv.at[0, pl.ds(0, sent)],
            dst_ref=kv.at[step, pl.ds(0, sent)],
            send_sem=kv_send.at[step],
            recv_sem=kv_recv.at[step],
            device_id=inner_id(step),
            device_id_type=MESH,
        )

    def forward(step):
        return pltpu.make_async_remote_copy(
            src_ref=kv.at[step, pl.ds(0, sent)],
            dst_ref=kv.at[step + 1, pl.ds(0, sent)],
            send_sem=kv_send.at[step + 1],
            recv_sem=kv_recv.at[step + 1],
            device_id=inner_id(1),
            device_id_type=MESH,
        )

    def pair_copy(g):
        return pltpu.make_async_remote_copy(
            src_ref=pair_out.at[g],
            dst_ref=pair_in.at[g],
            send_sem=pair_send.at[g],
            recv_sem=pair_recv.at[g],
            device_id=inner_id(1),
            device_id_type=MESH,
        )

    def part_copy(step):
        return pltpu.make_async_remote_copy(
            src_ref=part_out.at[step],
            dst_ref=part_in.at[step],
            send_sem=part_send.at[step],
            recv_sem=part_recv.at[step],
            device_id=inner_id(step),
            device_id_type=MESH,
        )

    groups = inners // 2
    direct = [1] + [2 * g for g in range(1, groups)]
    for load in loads[3:]:
        load.wait()
    row8 = lax.broadcasted_iota(jnp.int32, (8, tokens), 0)
    seg8 = jnp.broadcast_to(seg, (8, tokens))
    masks = jnp.where((row8 == 3) & (seg8 != 1.0), MASKED, 0.0)
    masks = jnp.where((row8 == 4) & (seg8 != 2.0), MASKED, masks)
    lane = lax.broadcasted_iota(jnp.int32, (tokens, HEAD_DIM), 1)
    def head_at(g):
        return (
            pl.ds(pl.multiple_of(g * tokens, tokens), tokens),
            pl.ds(pl.multiple_of(g * HEAD_DIM, HEAD_DIM), HEAD_DIM),
        )

    def prepare(g, carry):
        here, cols = head_at(g)
        query = q_ref[:, cols]
        grad = go_ref[:, cols]
        q_aug[here, :HEAD_DIM] = query
        go_aug[here, :HEAD_DIM] = grad
        high, middle, low = pieces(norm_ref[g] * -ROOT)
        top = jnp.where(row8 == 0, high, masks)
        top = jnp.where(row8 == 1, middle, top)
        top = jnp.where(row8 == 2, low, top)
        full = jnp.concatenate([top, jnp.zeros((HEAD_DIM - 8, tokens), F32)], axis=0)
        q_aug[here, HEAD_DIM:] = jnp.transpose(full).astype(BF16)
        delta = -jnp.sum(
            grad.astype(F32) * ao_ref[:, cols].astype(F32), axis=1, keepdims=True
        )
        d_high, d_middle, d_low = pieces(delta)
        side = jnp.where(lane == 0, d_high, 0.0)
        side = jnp.where(lane == 1, d_middle, side)
        side = jnp.where(lane == 2, d_low, side)
        go_aug[here, HEAD_DIM:] = side.astype(BF16)
        return carry

    lax.fori_loop(0, GROUP, prepare, 0)

    half = HEAD_DIM // 2
    for slot in range(inners):
        angles[slot : slot + 1] = starts_ref[pl.ds(partner(me, slot, inners), 1)]

    def both(table):
        below = lax.broadcasted_iota(jnp.int32, table.shape, 1) < half
        turned = pltpu.roll(table, half, 1)
        return jnp.where(below, turned, table), jnp.where(below, table, -turned)

    base_cos, base_sin = both(base_ref[...])
    start_cos, start_sin = both(angles[...])
    cosine = base_cos * start_cos[:1] - base_sin * start_sin[:1]
    sine = base_sin * start_cos[:1] + base_cos * start_sin[:1]
    base_turned = pltpu.roll(base_ref[...], half, 1)

    def waves(slot):
        start_cos, start_sin = both(angles[pl.ds(slot, 1)])
        return (base_ref[...] * start_cos + base_turned * start_sin).astype(BF16)

    def unrotate(x):
        return x * cosine + pltpu.roll(x, half, 1) * sine

    chunk = rows if tokens <= 128 else 256
    starts = list(range(0, rows, chunk))

    tile = 32

    def query_side(g):
        block = jnp.concatenate([kv[2 * g], kv[2 * g + 1]], axis=1)
        values_t = jnp.concatenate([block[:HEAD_DIM], block[2 * HEAD_DIM :]], axis=0)
        keys_t = block[HEAD_DIM:]
        for start in starts:
            here = slice(start, min(start + chunk, rows))
            scores[here] = dot(q_aug[here], keys_t)
            pulls[here] = dot(go_aug[here], values_t)
        keys[g, :, :HEAD_DIM] = jnp.transpose(block[HEAD_DIM : 2 * HEAD_DIM])
        keys[g, :tokens, HEAD_DIM:] = waves(2 * g)
        keys[g, tokens:, HEAD_DIM:] = waves(2 * g + 1)

        def one_stretch(i, carry):
            for start in range(0, HEAD_DIM, tile):
                here = pl.ds(pl.multiple_of(i * HEAD_DIM + start, tile), tile)
                chances = jnp.exp(scores[here] * SCALE)
                probs[g, here] = chances.astype(BF16)
                grads[g, here] = (chances * pulls[here]).astype(BF16)
                chance_part = chances[:, :HEAD_DIM]
                for col in range(HEAD_DIM, 2 * tokens, HEAD_DIM):
                    chance_part = chance_part + chances[:, col : col + HEAD_DIM]
                prob_sums[here] += chance_part
            return carry

        lax.fori_loop(0, rows // HEAD_DIM, one_stretch, 0)

    def key_side(g):
        return dot(q_t[...], grads[g]), dot(go_t[...], probs[g])

    def turn_over(g, carry):
        here, cols = head_at(g)
        q_t[:, here] = jnp.transpose(q_ref[:, cols])
        go_t[:, here] = jnp.transpose(go_ref[:, cols])
        return carry

    def pass_on(g):
        kv_copy(2 * g).wait_recv()
        forward(2 * g).start()

    def give(g):
        key_part, value_part = key_side(g)
        pair_out[g, :HEAD_DIM] = key_part[:, tokens:].astype(BF16)
        pair_out[g, HEAD_DIM:] = value_part[:, tokens:].astype(BF16)
        pair_copy(g).start()
        kept[g, :HEAD_DIM] = key_part[:, :tokens]
        kept[g, HEAD_DIM:] = value_part[:, :tokens]

    def send_home(g):
        pair_copy(g).wait_recv()
        part_out[2 * g] = (kept[g] + pair_in[g].astype(F32)).astype(BF16)
        part_copy(2 * g).start()

    pl.semaphore_wait(barrier, inners + outers - 2)
    for step in direct:
        kv_copy(step).start()

    prob_sums[...] = jnp.zeros((rows, HEAD_DIM), F32)
    lax.fori_loop(0, GROUP, turn_over, 0)

    def one_group(g, carry):
        @pl.when(g == 0)
        def _():
            kv_copy(1).wait_recv()

        @pl.when(g > 0)
        def _():
            forward(2 * g).wait_recv()

        query_side(g)

        @pl.when(g == 0)
        def _():
            pass_on(1)

        @pl.when(g + 2 < groups)
        def _():
            pass_on(g + 2)

        return carry

    lax.fori_loop(0, groups, one_group, 0)

    every_key = jnp.concatenate([keys[g] for g in range(groups)], axis=0)
    for start in starts:
        here = slice(start, min(start + chunk, rows))
        every_grad = jnp.concatenate([grads[g, here] for g in range(groups)], axis=1)
        dq_acc[here] = dot(every_grad, every_key)
    bias_own[...] = jnp.zeros((BIAS_ROWS, HEAD_DIM), F32)
    def finish(g, carry):
        key_bias, value_bias = carry
        here, cols = head_at(g)
        full = unrotate(dq_acc[here, :HEAD_DIM] * SCALE)
        dq_ref[:, cols] = full.astype(BF16)
        bias_own[pl.ds(g, 1)] = jnp.sum(full, axis=0, keepdims=True)
        query = q_ref[:, cols].astype(F32)
        turn_cos, turn_sin = both(dq_acc[here, HEAD_DIM:])
        key_bias = key_bias + query * turn_cos + pltpu.roll(query, half, 1) * turn_sin
        weight = jnp.sum(prob_sums[here], axis=1, keepdims=True)
        value_bias = value_bias + weight * go_ref[:, cols].astype(F32)
        return key_bias, value_bias

    nothing = jnp.zeros((tokens, HEAD_DIM), F32)
    key_bias, value_bias = lax.fori_loop(0, GROUP, finish, (nothing, nothing))
    bias_own[GROUP : GROUP + 1] = jnp.sum(key_bias, axis=0, keepdims=True) * SCALE
    bias_own[GROUP + 1 : GROUP + 2] = jnp.sum(value_bias, axis=0, keepdims=True)

    def bias_copy(step, slot):
        return pltpu.make_async_remote_copy(
            src_ref=bias_own,
            dst_ref=bias_in.at[slot],
            send_sem=bias_send.at[step],
            recv_sem=bias_recv.at[step],
            device_id=inner_id(step),
            device_id_type=MESH,
        )

    def plane_copy(step, slot):
        return pltpu.make_async_remote_copy(
            src_ref=plane_own,
            dst_ref=plane_in.at[slot],
            send_sem=plane_send.at[step],
            recv_sem=plane_recv.at[step],
            device_id=outer_id(step),
            device_id_type=MESH,
        )

    def bias_along():
        for step in range(1, inners):
            bias_copy(step, partner(me, step, inners)).wait_recv()
        summed = bias_in[0]
        for slot in range(1, inners):
            summed = summed + bias_in[slot]
        plane_own[...] = summed
        for step in range(1, outers):
            plane_copy(step, plane).start()
        plane_in[plane] = summed

    for step in range(1, inners):
        bias_copy(step, me).start()
    stores[0].start()
    bias_in[me] = bias_own[...]

    def one_gift(g, carry):
        give(g)

        @pl.when(g > 1)
        def _():
            send_home(g - 1)

        return carry

    lax.fori_loop(1, groups, one_gift, 0)
    bias_along()
    key_part, value_part = key_side(0)
    part_out[1, :HEAD_DIM] = key_part[:, tokens:].astype(BF16)
    part_out[1, HEAD_DIM:] = value_part[:, tokens:].astype(BF16)
    part_copy(1).start()
    send_home(groups - 1)
    own_acc[:HEAD_DIM] = key_part[:, :tokens]
    own_acc[HEAD_DIM:] = value_part[:, :tokens]

    total = own_acc[...]
    for step in direct:
        part_copy(step).wait_recv()
        total = total + part_in[step].astype(F32)
    key_full = unrotate(jnp.transpose(total[:HEAD_DIM]) * SCALE)
    value_full = jnp.transpose(total[HEAD_DIM:])
    dk_ref[...] = key_full.astype(BF16)
    dv_ref[...] = value_full.astype(BF16)
    stores[1].start()
    stores[2].start()

    for step in range(1, outers):
        plane_copy(step, partner(plane, step, outers)).wait_recv()
    for head in range(KV_HEADS):
        whole = plane_in[head]
        for other in range(head + KV_HEADS, outers, KV_HEADS):
            whole = whole + plane_in[other]
        bias_ref[head * GROUP : (head + 1) * GROUP] = whole[:GROUP]
        bias_ref[HEADS + head : HEADS + head + 1] = whole[GROUP : GROUP + 1]
        at = HEADS + KV_HEADS + head
        bias_ref[at : at + 1] = whole[GROUP + 1 : GROUP + 2]
    stores[3].start()

    for step in direct:
        kv_copy(step).wait_send()
        part_copy(step).wait_send()
    for g in range(1, groups):
        forward(2 * g).wait_send()
        pair_copy(g).wait_send()
    for step in range(1, inners):
        bias_copy(step, me).wait_send()
    for step in range(1, outers):
        plane_copy(step, plane).wait_send()
    for store in stores:
        store.wait()


def write(*refs):
    sources, targets, held, sem = refs[:4], refs[4:8], refs[8:12], refs[12]
    loads = [pltpu.make_async_copy(sources[i], held[i], sem.at[i]) for i in range(4)]
    stores = [pltpu.make_async_copy(held[i], targets[i], sem.at[4 + i]) for i in range(4)]
    for load in loads:
        load.start()
    for load, store in zip(loads, stores):
        load.wait()
        store.start()
    for store in stores:
        store.wait()


def rotary(positions):
    frequency = np.exp(np.arange(HEAD_DIM // 2) * (-2.0 * math.log(ROPE_BASE) / HEAD_DIM))
    angles = np.asarray(positions)[:, None] * frequency[None, :]
    return np.concatenate([np.sin(angles), np.cos(angles)], axis=1).astype(np.float32)


def local(inners, outers, query_rot, key_rot, value_rows, attention_out, grad_out, log_norm,
          segments, block_table):
    del block_table
    tokens = query_rot.shape[1]
    rows = GROUP * tokens
    if segments.shape[0] > 1:
        example = lax.axis_index("outer") // KV_HEADS
        segments = lax.dynamic_slice_in_dim(segments, example, 1, 0)
    hbm = pl.BlockSpec(memory_space=pltpu.HBM)
    sems = pltpu.SemaphoreType.DMA
    shapes = (
        jax.ShapeDtypeStruct((tokens, GROUP * HEAD_DIM), BF16),
        jax.ShapeDtypeStruct((tokens, HEAD_DIM), BF16),
        jax.ShapeDtypeStruct((tokens, HEAD_DIM), BF16),
        jax.ShapeDtypeStruct((HEADS + 2 * KV_HEADS, HEAD_DIM), F32),
    )
    outs = pl.pallas_call(
        functools.partial(kernel, inners, outers),
        out_shape=shapes,
        in_specs=[hbm] * 9,
        out_specs=(hbm,) * 4,
        scratch_shapes=[
            pltpu.VMEM((tokens, HEAD_DIM), BF16),
            pltpu.VMEM((tokens, HEAD_DIM), BF16),
            pltpu.VMEM((1, tokens), jnp.int32),
            pltpu.VMEM((tokens, GROUP * HEAD_DIM), BF16),
            pltpu.VMEM((tokens, GROUP * HEAD_DIM), BF16),
            pltpu.VMEM((tokens, GROUP * HEAD_DIM), BF16),
            pltpu.VMEM((GROUP, 1, tokens), F32),
            pltpu.VMEM((tokens, HEAD_DIM), F32),
            pltpu.VMEM((inners, HEAD_DIM), F32),
            sems((9,)),
            pltpu.VMEM((tokens, GROUP * HEAD_DIM), BF16),
            pltpu.VMEM((tokens, HEAD_DIM), BF16),
            pltpu.VMEM((tokens, HEAD_DIM), BF16),
            pltpu.VMEM((HEADS + 2 * KV_HEADS, HEAD_DIM), F32),
            sems((4,)),
            pltpu.VMEM((inners, 3 * HEAD_DIM, tokens), BF16),
            pltpu.VMEM((rows, 2 * HEAD_DIM), BF16),
            pltpu.VMEM((rows, 2 * HEAD_DIM), BF16),
            pltpu.VMEM((HEAD_DIM, rows), BF16),
            pltpu.VMEM((HEAD_DIM, rows), BF16),
            pltpu.VMEM((inners // 2, rows, 2 * tokens), BF16),
            pltpu.VMEM((inners // 2, rows, 2 * tokens), BF16),
            pltpu.VMEM((rows, 2 * tokens), F32),
            pltpu.VMEM((rows, 2 * tokens), F32),
            pltpu.VMEM((inners // 2, 2 * tokens, 2 * HEAD_DIM), BF16),
            pltpu.VMEM((rows, 2 * HEAD_DIM), F32),
            pltpu.VMEM((2 * HEAD_DIM, tokens), F32),
            pltpu.VMEM((inners // 2, 2 * HEAD_DIM, tokens), F32),
            pltpu.VMEM((inners // 2, 2 * HEAD_DIM, tokens), BF16),
            pltpu.VMEM((inners // 2, 2 * HEAD_DIM, tokens), BF16),
            pltpu.VMEM((inners, 2 * HEAD_DIM, tokens), BF16),
            pltpu.VMEM((inners, 2 * HEAD_DIM, tokens), BF16),
            pltpu.VMEM((rows, HEAD_DIM), F32),
            pltpu.VMEM((inners, HEAD_DIM), F32),
            pltpu.VMEM((BIAS_ROWS, HEAD_DIM), F32),
            pltpu.VMEM((inners, BIAS_ROWS, HEAD_DIM), F32),
            pltpu.VMEM((BIAS_ROWS, HEAD_DIM), F32),
            pltpu.VMEM((outers, BIAS_ROWS, HEAD_DIM), F32),
            sems((inners,)), sems((inners,)), sems((inners // 2,)), sems((inners // 2,)),
            sems((inners,)), sems((inners,)),
            sems((inners,)), sems((inners,)), sems((outers,)), sems((outers,)),
        ],
        compiler_params=pltpu.CompilerParams(
            collective_id=0, has_side_effects=True, vmem_limit_bytes=VMEM_LIMIT
        ),
        name="attention_backward",
    )(
        key_rot[0], value_rows[0], segments, query_rot[0], grad_out[0], attention_out[0],
        log_norm.reshape(GROUP, 1, tokens), jnp.asarray(rotary(np.arange(tokens))),
        jnp.asarray(rotary(np.arange(inners) * tokens)),
    )
    outs = pl.pallas_call(
        write,
        out_shape=shapes,
        in_specs=[hbm] * 4,
        out_specs=(hbm,) * 4,
        scratch_shapes=[pltpu.VMEM(shape.shape, shape.dtype) for shape in shapes] + [sems((8,))],
        compiler_params=pltpu.CompilerParams(vmem_limit_bytes=VMEM_LIMIT),
        name="write_results",
    )(*outs)
    return outs[0][None], outs[1][None], outs[2][None], outs[3].reshape(-1)


def solution(mesh):
    placed = (
        P("outer", "inner", None),
        P("outer", "inner", None),
        P("outer", "inner", None),
        P("outer", "inner", None),
        P("outer", "inner", None),
        P("outer", None, "inner"),
        P(None, "inner"),
        P(None, "inner", None),
    )
    return jax.shard_map(
        functools.partial(local, mesh.shape["inner"], mesh.shape["outer"]),
        mesh=mesh,
        in_specs=placed,
        out_specs=(
            P("outer", "inner", None),
            P("outer", "inner", None),
            P("outer", "inner", None),
            P(),
        ),
        check_vma=False,
    )
```
